512 devices in a mesh: seq: 128 (over z, y, core), chan: 4 (over x).
Axes of the slice: x: 4, y: 8, z: 8, core: 2. Of those that a mesh axis runs over, the one named last changes fastest.
Arguments:
- values: bfloat16 [160, 128, 4096], P(None, 'seq', 'chan'), may hold values from -6 to 6
- gates: bfloat16 [160, 128, 4096], P(None, 'seq', 'chan'), may hold values from -6 to 6
- filters: bfloat16 [256, 4096], P(None, 'chan'), may hold values from -1.1 to 1.1
- skip: float32 [4096], P('chan'), may hold values from -1 to 1
- weights: bfloat16 [4096, 4096], P(None, ('chan', 'seq')), may hold values from -0.09375 to 0.09375
- doc_lengths: int32 [128], replicated, may hold values from 1 to 256, 20480 in all
Outputs:
- mixed: bfloat16 [160, 128, 4096], P(None, 'seq', 'chan')
The draws below stay inside these ranges and needn't reach their ends.
Inputs may be any that keep to these rules, and one draw needn't show every extreme that they name: `doc_lengths`: the 128 documents lie in order and together fill the 20480 rows of the window; the longest has exactly 256 rows.
All inputs are finite; a program needn't handle non-finite values.
Results may differ from the reference program's by a relative error of at most 0.0057.
Values may be sent and summed in bfloat16 or wider, within the bound.
No kernel may reach another device: no remote copies, remote signals or barrier semaphores. Data moves between devices by JAX's collectives and lax.ppermute only.
A program may use at most 64 MiB of HBM per device.

```python
import math
import jax
import jax.numpy as jnp
import numpy as np
from jax import lax

D = 4096
SLOT = 256
TOK_DEV = 160
SHARDS = 128
TOKENS = 20480


def draw_filters(key, part):
    key = jax.random.fold_in(key, 7)
    noise_key, span_key = jax.random.split(key)
    taps = jnp.arange(SLOT, dtype=jnp.float32)[:, None]
    shortest = 30.0
    longest = SLOT * 4.0
    noise = jnp.clip(jax.random.normal(noise_key, (SLOT, D), jnp.float32), -4.0, 4.0)
    decay_span = jnp.exp(jax.random.uniform(span_key, (1, D), jnp.float32, math.log(shortest), math.log(longest)))
    shaped = noise * jnp.exp(-taps / decay_span) * jnp.sqrt(2.0 / decay_span)
    return shaped.astype(jnp.bfloat16)


def block_scale(own_key, dims, cuts, smallest, largest):
    def one(position, parts):
        heights = jax.random.uniform(jax.random.fold_in(jax.random.fold_in(own_key, 6), position), (parts,), jnp.float32, smallest / len(cuts), largest / len(cuts))
        return jnp.repeat(jnp.exp(heights), dims[position] // parts).reshape((-1,) + (1,) * (len(dims) - position - 1))

    gain = one(*cuts[0])
    for cut in cuts[1:]:
        gain = gain * one(*cut)
    return gain


def profile(amount, total, most, skew):
    loads = [(1 << 20) // math.isqrt(standing ** skew) + 1 for standing in range(2, amount + 1)]
    spare, given = total - most - (amount - 1), [1] * (amount - 1)
    while spare > 0:
        candidates = [i for i in range(amount - 1) if given[i] < most]
        whole, left = sum([loads[i] for i in candidates]), spare
        for i in candidates:
            more = min(most - given[i], max(1, left * loads[i] // whole), spare)
            given[i] = given[i] + more
            spare = spare - more
    return np.array([most] + given)


def ragged(rng, number_of, total, bound, lean):
    if number_of == 2:
        one = jax.random.randint(rng, (), max(1, total - bound), min(bound, total - 1) + 1)
        return jnp.stack([one, total - one])
    tallies = jnp.asarray(profile(number_of, total, bound, lean), jnp.int32)
    twos = (number_of - 1) // 2
    donor, taker = tallies[1:1 + 2 * twos:2], tallies[2:2 + 2 * twos:2]
    room = jnp.minimum(donor - 1, bound - taker)
    shifted = jax.random.randint(jax.random.fold_in(rng, 1), (twos,), 0, 1 << 20) % (room + 1)
    tallies = tallies.at[1:1 + 2 * twos:2].set(donor - shifted).at[2:2 + 2 * twos:2].set(taker + shifted)
    return tallies[jax.random.permutation(jax.random.fold_in(rng, 2), number_of)]


def centred(stream_key, dims, scale, reach, cuts=(), kind=jnp.bfloat16):
    array = jax.random.normal(stream_key, dims, jnp.float32) * scale
    if len(cuts) > 0:
        array = block_scale(stream_key, dims, cuts, -0.22, 0.18) * array
    return jnp.clip(array, min=-reach, max=reach).astype(kind)


def setup_inputs(seed: int = 0) -> dict:
    seeds = jax.random.split(jax.random.key(seed), 7)
    values = centred(seeds[0], (TOK_DEV, SHARDS, D), 1.0, 6.0, ((1, 128), (2, 4)))
    gates = centred(seeds[1], (TOK_DEV, SHARDS, D), 1.0, 6.0, ((1, 128), (2, 4)))
    filters = draw_filters(jax.random.fold_in(seeds[6], 71), 0)
    skip = jnp.clip(jax.random.uniform(seeds[3], (D,), jnp.float32, -1.0, 1.0) * block_scale(seeds[3], (D,), ((0, 4),), -0.4, 0.0), -1.0, 1.0)
    weights = centred(seeds[4], (D, D), D ** -0.5, 0.09375, ((1, 512),))
    doc_lengths = ragged(seeds[5], SHARDS, TOKENS, SLOT, 2).astype(jnp.int32)
    return {"values": values, "gates": gates, "filters": filters, "skip": skip, "weights": weights, "doc_lengths": doc_lengths}


def reference(values, gates, filters, skip, weights, doc_lengths):
    flat_values = values.reshape(TOKENS, D).astype(jnp.float32)
    padded = jnp.concatenate([flat_values, jnp.zeros((SLOT, D), jnp.float32)], axis=0)
    spectrum = jnp.fft.rfft(filters.astype(jnp.float32), n=2 * SLOT, axis=0)
    starts = (jnp.cumsum(doc_lengths) - doc_lengths).astype(jnp.int32)
    positions = jnp.arange(SLOT, dtype=jnp.int32)[:, None]

    def one_doc(carry, doc_item):
        doc_start, doc_length = doc_item
        segment = lax.dynamic_slice(padded, (doc_start, jnp.int32(0)), (SLOT, D))
        present = positions < doc_length
        segment = jnp.where(present, segment, 0.0)
        conv_out = jnp.fft.irfft(jnp.fft.rfft(segment, n=2 * SLOT, axis=0) * spectrum, n=2 * SLOT, axis=0)[:SLOT]
        result = (conv_out + skip[None, :] * segment).astype(jnp.bfloat16)
        previous = lax.dynamic_slice(carry, (doc_start, jnp.int32(0)), (SLOT, D))
        return lax.dynamic_update_slice(carry, jnp.where(present, result, previous), (doc_start, jnp.int32(0))), None

    carry = jnp.zeros((TOKENS + SLOT, D), jnp.bfloat16)
    convolved, _ = lax.scan(one_doc, carry, (starts, doc_lengths.astype(jnp.int32)))
    convolved = convolved[:TOKENS]
    gated = (gates.reshape(TOKENS, D).astype(jnp.float32) * convolved.astype(jnp.float32)).astype(jnp.bfloat16)
    mixed = jnp.dot(gated, weights, preferred_element_type=jnp.float32).astype(jnp.bfloat16)
    return mixed.reshape(TOK_DEV, SHARDS, D)
```

```python
import functools

import jax
import jax.numpy as jnp
from jax import lax
from jax.experimental import pallas as pl
from jax.experimental.pallas import tpu as pltpu
from jax.sharding import Mesh
from jax.sharding import PartitionSpec as P

F32 = jnp.float32
BF16 = jnp.bfloat16
LANES = 128
CH = 8
ROWS = 160
HEAD = 128
TAIL = ROWS - HEAD
FOLD = LANES // TAIL
PER = CH + CH // FOLD
PEERS = 128
MSG = PEERS * PER
VMEM_LIMIT = 48 * 1024 * 1024
SEQ = ("z", "y", "core")


def full(shape):
    return pl.BlockSpec(shape, lambda: (0,) * len(shape))


def call(kernel, out, ins, scratch, flops=0, smem=0):
    args = ins
    in_specs = [pl.BlockSpec(memory_space=pltpu.SMEM)] * smem
    in_specs += [full(a.shape) for a in args[smem:]]
    nbytes = sum(a.size * a.dtype.itemsize for a in args)
    nbytes += out.size * out.dtype.itemsize
    return pl.pallas_call(
        kernel,
        out_shape=out,
        in_specs=in_specs,
        out_specs=full(out.shape),
        scratch_shapes=scratch,
        compiler_params=pltpu.CompilerParams(vmem_limit_bytes=VMEM_LIMIT),
        cost_estimate=pl.CostEstimate(flops=flops, bytes_accessed=nbytes, transcendentals=0),
    )(*args)


def pack_kernel(v_ref, out_ref, msg, low):
    for j in range(8):
        cols = slice(j * LANES, (j + 1) * LANES)
        block = v_ref[:, cols].astype(F32)
        head = block[:HEAD].T
        for g in range(16):
            msg[pl.ds((16 * j + g) * PER, CH), :] = head[g * CH : (g + 1) * CH]
        low[cols, :TAIL] = block[HEAD:].T
    for i in range(CH // FOLD):
        parts = [low[pl.ds(FOLD * i + k, PEERS, stride=CH), :][:, :TAIL] for k in range(FOLD)]
        msg[pl.ds(CH + i, PEERS, stride=PER), :] = jnp.concatenate(parts, axis=1)
    out_ref[...] = msg[...].astype(BF16)


def toeplitz_kernel(index_ref, f_ref, out_ref, taps):
    group = index_ref[0]
    tile = pl.multiple_of(lax.div(group, 16) * LANES, LANES)
    taps[...] = f_ref[:, pl.ds(tile, LANES)].astype(F32).T
    mine = taps[pl.ds(pl.multiple_of(lax.rem(group, 16) * CH, CH), CH), :]
    row = lax.broadcasted_iota(jnp.int32, (LANES, LANES), 0)
    lane = lax.broadcasted_iota(jnp.int32, (LANES, LANES), 1)
    for c in range(CH):
        spread = jnp.broadcast_to(mine[c : c + 1, :], (LANES, 2 * LANES))
        turned = pltpu.roll(spread, 0, 1, stride=1, stride_axis=0)
        near = jnp.where(lane >= row, turned[:, :LANES], 0.0).astype(BF16)
        out_ref[c, :LANES, :LANES] = near
        out_ref[c, LANES:, LANES:] = near
        out_ref[c, :LANES, LANES:] = turned[:, LANES:].astype(BF16)
        out_ref[c, LANES:, :LANES] = jnp.zeros((LANES, LANES), BF16)


def conv_kernel(start_ref, length_ref, skip_ref, in_ref, toep_ref, out_ref, msg, seq, result, first, second):
    msg[...] = in_ref[...].astype(F32)
    for c in range(CH):
        seq[pl.ds(c, HEAD, stride=CH), :] = msg[pl.ds(c, PEERS, stride=PER), :].T
    for i in range(CH // FOLD):
        tail = msg[pl.ds(CH + i, PEERS, stride=PER), :].T
        for k in range(FOLD):
            seq[pl.ds(HEAD * CH + FOLD * i + k, TAIL, stride=CH), :] = tail[k * TAIL : (k + 1) * TAIL]
    result[...] = jnp.zeros_like(result)
    lane = lax.broadcasted_iota(jnp.int32, (CH, LANES), 1)

    def take(d, carry):
        begin, length = start_ref[d], length_ref[d]
        row = pl.multiple_of(lax.shift_right_logical(begin, 7) * CH, CH)
        turn = begin & (LANES - 1)
        back = (LANES - turn) & (LANES - 1)
        pieces = [pltpu.roll(seq[pl.ds(row + CH * i, CH), :], back, 1) for i in range(3)]
        whole = lane < LANES - turn
        near = jnp.where(whole, pieces[0], pieces[1])
        far = jnp.where(whole, pieces[1], pieces[2])
        first[pl.ds(d, CH, stride=PEERS), :] = jnp.where(lane < length, near, 0.0)
        second[pl.ds(d, CH, stride=PEERS), :] = jnp.where(lane < length - LANES, far, 0.0)
        return carry

    lax.fori_loop(0, PEERS, take, 0, unroll=8)
    for c in range(CH):
        rows = slice(c * PEERS, (c + 1) * PEERS)
        near, far = first[rows, :], second[rows, :]
        both = jnp.concatenate([near, far], axis=1).astype(BF16)
        done = jnp.dot(both, toep_ref[c], preferred_element_type=F32)
        gain = skip_ref[c]
        first[rows, :] = (done[:, :LANES] + gain * near).astype(BF16).astype(F32)
        second[rows, :] = (done[:, LANES:] + gain * far).astype(BF16).astype(F32)

    def give(d, carry):
        begin, length = start_ref[d], length_ref[d]
        row = pl.multiple_of(lax.shift_right_logical(begin, 7) * CH, CH)
        turn = begin & (LANES - 1)
        near = jnp.where(lane < length, first[pl.ds(d, CH, stride=PEERS), :], 0.0)
        far = jnp.where(lane < length - LANES, second[pl.ds(d, CH, stride=PEERS), :], 0.0)
        near = pltpu.roll(near, turn, 1)
        far = pltpu.roll(far, turn, 1)
        whole = lane >= turn
        result[pl.ds(row, CH), :] += jnp.where(whole, near, 0.0)
        result[pl.ds(row + CH, CH), :] += jnp.where(whole, far, near)
        result[pl.ds(row + 2 * CH, CH), :] += jnp.where(whole, 0.0, far)
        return carry

    lax.fori_loop(0, PEERS, give, 0, unroll=8)
    for c in range(CH):
        msg[pl.ds(c, PEERS, stride=PER), :] = result[pl.ds(c, HEAD, stride=CH), :].T
    for i in range(CH // FOLD):
        parts = [result[pl.ds(HEAD * CH + FOLD * i + k, TAIL, stride=CH), :] for k in range(FOLD)]
        msg[pl.ds(CH + i, PEERS, stride=PER), :] = jnp.concatenate(parts, axis=0).T
    out_ref[...] = msg[...].astype(BF16)


def gate_kernel(in_ref, g_ref, out_ref, msg, low):
    msg[...] = in_ref[...].astype(F32)
    for i in range(CH // FOLD):
        tail = msg[pl.ds(CH + i, PEERS, stride=PER), :]
        for k in range(FOLD):
            low[pl.ds(FOLD * i + k, PEERS, stride=CH), :TAIL] = tail[:, k * TAIL : (k + 1) * TAIL]
    for j in range(8):
        cols = slice(j * LANES, (j + 1) * LANES)
        head = [msg[pl.ds((16 * j + g) * PER, CH), :] for g in range(16)]
        head = jnp.concatenate(head, axis=0).T
        out_ref[:HEAD, cols] = (head * g_ref[:HEAD, cols].astype(F32)).astype(BF16)
        tail = low[cols, :].T[:TAIL]
        out_ref[HEAD:, cols] = (tail * g_ref[HEAD:, cols].astype(F32)).astype(BF16)


def exchange(message):
    sent = message.reshape(PEERS, PER // 2, 2, LANES)
    got = lax.all_to_all(sent, SEQ, split_axis=0, concat_axis=0, tiled=True)
    return got.reshape(MSG, LANES)


def local(values, gates, filters, skip, weights, doc_lengths):
    index = lax.axis_index(SEQ).astype(jnp.int32)
    width = values.shape[2]
    msg = jax.ShapeDtypeStruct((MSG, LANES), BF16)
    buf = pltpu.VMEM((MSG, LANES), F32)
    low = pltpu.VMEM((width, LANES), F32)
    packed = call(pack_kernel, msg, [values.reshape(ROWS, width)], [buf, low])
    toep = call(
        toeplitz_kernel,
        jax.ShapeDtypeStruct((CH, 2 * LANES, 2 * LANES), BF16),
        [index[None], filters],
        [pltpu.VMEM((LANES, 2 * LANES), F32)],
        smem=1,
    )
    starts = jnp.cumsum(doc_lengths) - doc_lengths
    own_skip = lax.dynamic_slice(skip, (index * CH,), (CH,))
    got = exchange(packed)
    convolved = call(
        conv_kernel,
        msg,
        [starts, doc_lengths, own_skip, got, toep],
        [
            buf,
            pltpu.VMEM((MSG + 3 * CH, LANES), F32),
            pltpu.VMEM((MSG + 3 * CH, LANES), F32),
            pltpu.VMEM((CH * PEERS, LANES), F32),
            pltpu.VMEM((CH * PEERS, LANES), F32),
        ],
        flops=2 * CH * PEERS * 256 * 256,
        smem=3,
    )
    back = exchange(convolved)
    gated = call(
        gate_kernel,
        jax.ShapeDtypeStruct((ROWS, width), BF16),
        [back, gates.reshape(ROWS, width)],
        [buf, low],
    )
    return project(gated, weights, index)


def project(gated, weights, index):
    half = gated.shape[1] // 2
    parts = [lax.all_gather(gated[:, a : a + half], "chan", axis=0) for a in (0, half)]
    rows = jnp.concatenate(parts, axis=2)
    rows = jnp.swapaxes(rows, 0, 1).reshape(ROWS, -1)
    table = lax.all_gather(weights.T, SEQ, axis=0, tiled=True)
    mixed = lax.dot_general(rows, table, (((1,), (1,)), ((), ())), preferred_element_type=F32)
    return mixed.astype(BF16)[:, None, :]


def solution(mesh):
    shape = dict(z=8, y=8, core=2, chan=4)
    fine = Mesh(mesh.devices.reshape(tuple(shape.values())), tuple(shape))
    placed = (
        P(None, SEQ, "chan"),
        P(None, SEQ, "chan"),
        P(None, "chan"),
        P("chan"),
        P(None, ("chan",) + SEQ),
        P(),
    )
    return jax.shard_map(
        local, mesh=fine, in_specs=placed, out_specs=P(None, SEQ, "chan"), check_vma=False
    )
```

```python
import functools

import jax
import jax.numpy as jnp
from jax import lax
from jax.experimental import pallas as pl
from jax.experimental.pallas import tpu as pltpu
from jax.sharding import PartitionSpec as P

F32 = jnp.float32
BF16 = jnp.bfloat16
LANES = 128
CH = 8
ROWS = 160
HEAD = 128
TAIL = ROWS - HEAD
FOLD = LANES // TAIL
PER = CH + CH // FOLD
PEERS = 128
MSG = PEERS * PER
VMEM_LIMIT = 48 * 1024 * 1024
SEQ = "seq"


def full(shape):
    return pl.BlockSpec(shape, lambda: (0,) * len(shape))


def call(kernel, out, ins, scratch, flops=0, smem=0):
    args = ins
    in_specs = [pl.BlockSpec(memory_space=pltpu.SMEM)] * smem
    in_specs += [full(a.shape) for a in args[smem:]]
    nbytes = sum(a.size * a.dtype.itemsize for a in args)
    nbytes += out.size * out.dtype.itemsize
    return pl.pallas_call(
        kernel,
        out_shape=out,
        in_specs=in_specs,
        out_specs=full(out.shape),
        scratch_shapes=scratch,
        compiler_params=pltpu.CompilerParams(vmem_limit_bytes=VMEM_LIMIT),
        cost_estimate=pl.CostEstimate(flops=flops, bytes_accessed=nbytes, transcendentals=0),
    )(*args)


def pack_kernel(v_ref, out_ref, msg, low):
    for j in range(8):
        cols = slice(j * LANES, (j + 1) * LANES)
        block = v_ref[:, cols].astype(F32)
        head = block[:HEAD].T
        for g in range(16):
            msg[pl.ds((16 * j + g) * PER, CH), :] = head[g * CH : (g + 1) * CH]
        low[cols, :TAIL] = block[HEAD:].T
    for i in range(CH // FOLD):
        parts = [low[pl.ds(FOLD * i + k, PEERS, stride=CH), :][:, :TAIL] for k in range(FOLD)]
        msg[pl.ds(CH + i, PEERS, stride=PER), :] = jnp.concatenate(parts, axis=1)
    out_ref[...] = msg[...].astype(BF16)


def toeplitz_kernel(index_ref, f_ref, out_ref, taps):
    group = index_ref[0]
    tile = pl.multiple_of(lax.div(group, 16) * LANES, LANES)
    taps[...] = f_ref[:, pl.ds(tile, LANES)].astype(F32).T
    mine = taps[pl.ds(pl.multiple_of(lax.rem(group, 16) * CH, CH), CH), :]
    row = lax.broadcasted_iota(jnp.int32, (LANES, LANES), 0)
    lane = lax.broadcasted_iota(jnp.int32, (LANES, LANES), 1)
    for c in range(CH):
        spread = jnp.broadcast_to(mine[c : c + 1, :], (LANES, 2 * LANES))
        turned = pltpu.roll(spread, 0, 1, stride=1, stride_axis=0)
        near = jnp.where(lane >= row, turned[:, :LANES], 0.0).astype(BF16)
        out_ref[c, :LANES, :LANES] = near
        out_ref[c, LANES:, LANES:] = near
        out_ref[c, :LANES, LANES:] = turned[:, LANES:].astype(BF16)
        out_ref[c, LANES:, :LANES] = jnp.zeros((LANES, LANES), BF16)


def conv_kernel(start_ref, length_ref, skip_ref, in_ref, toep_ref, out_ref, msg, seq, result, first, second):
    msg[...] = in_ref[...].astype(F32)
    for c in range(CH):
        seq[pl.ds(c, HEAD, stride=CH), :] = msg[pl.ds(c, PEERS, stride=PER), :].T
    for i in range(CH // FOLD):
        tail = msg[pl.ds(CH + i, PEERS, stride=PER), :].T
        for k in range(FOLD):
            seq[pl.ds(HEAD * CH + FOLD * i + k, TAIL, stride=CH), :] = tail[k * TAIL : (k + 1) * TAIL]
    result[...] = jnp.zeros_like(result)
    lane = lax.broadcasted_iota(jnp.int32, (CH, LANES), 1)

    def take(d, carry):
        begin, length = start_ref[d], length_ref[d]
        row = pl.multiple_of(lax.shift_right_logical(begin, 7) * CH, CH)
        turn = begin & (LANES - 1)
        back = (LANES - turn) & (LANES - 1)
        pieces = [pltpu.roll(seq[pl.ds(row + CH * i, CH), :], back, 1) for i in range(3)]
        whole = lane < LANES - turn
        near = jnp.where(whole, pieces[0], pieces[1])
        far = jnp.where(whole, pieces[1], pieces[2])
        first[pl.ds(d, CH, stride=PEERS), :] = jnp.where(lane < length, near, 0.0)
        second[pl.ds(d, CH, stride=PEERS), :] = jnp.where(lane < length - LANES, far, 0.0)
        return carry

    lax.fori_loop(0, PEERS, take, 0, unroll=8)
    for c in range(CH):
        rows = slice(c * PEERS, (c + 1) * PEERS)
        near, far = first[rows, :], second[rows, :]
        both = jnp.concatenate([near, far], axis=1).astype(BF16)
        done = jnp.dot(both, toep_ref[c], preferred_element_type=F32)
        gain = skip_ref[c]
        first[rows, :] = (done[:, :LANES] + gain * near).astype(BF16).astype(F32)
        second[rows, :] = (done[:, LANES:] + gain * far).astype(BF16).astype(F32)

    def give(d, carry):
        begin, length = start_ref[d], length_ref[d]
        row = pl.multiple_of(lax.shift_right_logical(begin, 7) * CH, CH)
        turn = begin & (LANES - 1)
        near = jnp.where(lane < length, first[pl.ds(d, CH, stride=PEERS), :], 0.0)
        far = jnp.where(lane < length - LANES, second[pl.ds(d, CH, stride=PEERS), :], 0.0)
        near = pltpu.roll(near, turn, 1)
        far = pltpu.roll(far, turn, 1)
        whole = lane >= turn
        result[pl.ds(row, CH), :] += jnp.where(whole, near, 0.0)
        result[pl.ds(row + CH, CH), :] += jnp.where(whole, far, near)
        result[pl.ds(row + 2 * CH, CH), :] += jnp.where(whole, 0.0, far)
        return carry

    lax.fori_loop(0, PEERS, give, 0, unroll=8)
    for c in range(CH):
        msg[pl.ds(c, PEERS, stride=PER), :] = result[pl.ds(c, HEAD, stride=CH), :].T
    for i in range(CH // FOLD):
        parts = [result[pl.ds(HEAD * CH + FOLD * i + k, TAIL, stride=CH), :] for k in range(FOLD)]
        msg[pl.ds(CH + i, PEERS, stride=PER), :] = jnp.concatenate(parts, axis=0).T
    out_ref[...] = msg[...].astype(BF16)


def gate_kernel(in_ref, g_ref, out_ref, msg, low):
    msg[...] = in_ref[...].astype(F32)
    for i in range(CH // FOLD):
        tail = msg[pl.ds(CH + i, PEERS, stride=PER), :]
        for k in range(FOLD):
            low[pl.ds(FOLD * i + k, PEERS, stride=CH), :TAIL] = tail[:, k * TAIL : (k + 1) * TAIL]
    for j in range(8):
        cols = slice(j * LANES, (j + 1) * LANES)
        head = [msg[pl.ds((16 * j + g) * PER, CH), :] for g in range(16)]
        head = jnp.concatenate(head, axis=0).T
        head = (head * g_ref[:HEAD, cols].astype(F32)).astype(BF16)
        tail = low[cols, :].T[:TAIL]
        tail = (tail * g_ref[HEAD:, cols].astype(F32)).astype(BF16)
        for q in range(out_ref.shape[0]):
            out_ref[q, :HEAD, cols] = head
            out_ref[q, HEAD:, cols] = tail


def multiply(rows_ref, w_ref):
    groups, _, width = rows_ref.shape
    total = jnp.zeros((w_ref.shape[0], ROWS), F32)
    for q in range(groups):
        part = w_ref[:, q * width : (q + 1) * width]
        total += lax.dot_general(part, rows_ref[q], (((1,), (1,)), ((), ())), preferred_element_type=F32)
    return total


def own_kernel(rows_ref, w_ref, out_ref):
    out_ref[...] = multiply(rows_ref, w_ref)


def other_kernel(core_ref, rows_ref, w_ref, own_ref, out_ref, zy, yz):
    other = multiply(rows_ref, w_ref)
    own_first = core_ref[0] == 0
    own = own_ref[...]
    zy[...] = jnp.where(own_first, own, other)
    yz[...] = jnp.where(own_first, other, own)
    for z in range(8):
        parts = []
        for y in range(8):
            parts.append(zy[(8 * z + y) * 8 : (8 * z + y + 1) * 8, :])
            parts.append(yz[(8 * y + z) * 8 : (8 * y + z + 1) * 8, :])
        block = jnp.concatenate(parts, axis=0)
        out_ref[:, z * LANES : (z + 1) * LANES] = block.T.astype(BF16)


def exchange(message):
    sent = message.reshape(PEERS, PER // 2, 2, LANES)
    got = lax.all_to_all(sent, SEQ, split_axis=0, concat_axis=0, tiled=True)
    return got.reshape(MSG, LANES)


def local(values, gates, filters, skip, weights, doc_lengths):
    index = lax.axis_index(SEQ).astype(jnp.int32)
    width = values.shape[2]
    msg = jax.ShapeDtypeStruct((MSG, LANES), BF16)
    buf = pltpu.VMEM((MSG, LANES), F32)
    low = pltpu.VMEM((width, LANES), F32)
    line = gather_line(weights.T)
    packed = call(pack_kernel, msg, [values.reshape(ROWS, width)], [buf, low])
    packed, filters, doc_lengths, skip = lax.optimization_barrier((packed, filters, doc_lengths, skip))
    toep = call(
        toeplitz_kernel,
        jax.ShapeDtypeStruct((CH, 2 * LANES, 2 * LANES), BF16),
        [index[None], filters],
        [pltpu.VMEM((LANES, 2 * LANES), F32)],
        smem=1,
    )
    starts = jnp.cumsum(doc_lengths) - doc_lengths
    own_skip = lax.dynamic_slice(skip, (index * CH,), (CH,))
    got, line, toep, starts, own_skip = lax.optimization_barrier(
        (exchange(packed), line, toep, starts, own_skip)
    )
    own = lax.all_gather(line, "seq", axis=0, axis_index_groups=lines("z"), tiled=True)
    convolved = call(
        conv_kernel,
        msg,
        [starts, doc_lengths, own_skip, got, toep],
        [
            buf,
            pltpu.VMEM((MSG + 3 * CH, LANES), F32),
            pltpu.VMEM((MSG + 3 * CH, LANES), F32),
            pltpu.VMEM((CH * PEERS, LANES), F32),
            pltpu.VMEM((CH * PEERS, LANES), F32),
        ],
        flops=2 * CH * PEERS * 256 * 256,
        smem=3,
    )
    back, own = lax.optimization_barrier((exchange(convolved), own))
    other = lax.ppermute(own, "seq", [(i, i ^ 1) for i in range(PEERS)])
    groups = lax.axis_size("chan")
    copies = call(
        gate_kernel,
        jax.ShapeDtypeStruct((groups, ROWS, width), BF16),
        [back, gates.reshape(ROWS, width)],
        [buf, low],
    )
    rows = lax.all_to_all(copies, "chan", split_axis=0, concat_axis=0, tiled=True)
    half = jax.ShapeDtypeStruct((own.shape[0], ROWS), F32)
    place = pltpu.VMEM(half.shape, F32)
    flops = 2 * ROWS * own.size
    first = call(own_kernel, half, [rows, own], [], flops=flops)
    core = lax.rem(index, 2)[None]
    mixed = call(
        other_kernel,
        jax.ShapeDtypeStruct((ROWS, width), BF16),
        [core, rows, other, first],
        [place, place],
        flops=flops,
        smem=1,
    )
    return mixed[:, None, :]


def lines(first):
    along = {"y": [], "z": []}
    for core in range(2):
        axis = first if core == 0 else ("z" if first == "y" else "y")
        for fixed in range(8):
            along[axis].append([(fixed * 16 + i * 2 if axis == "y" else i * 16 + fixed * 2) + core for i in range(8)])
    return along["y"] + along["z"]


def gather_line(shard):
    twice = jnp.concatenate([shard, shard], axis=0)
    got = lax.all_gather(twice, "seq", axis=0, axis_index_groups=lines("y"))
    return got[:, : shard.shape[0]].reshape(-1, shard.shape[1])


def solution(mesh):
    placed = (
        P(None, "seq", "chan"),
        P(None, "seq", "chan"),
        P(None, "chan"),
        P("chan"),
        P(None, ("chan", "seq")),
        P(),
    )
    return jax.shard_map(
        local, mesh=mesh, in_specs=placed, out_specs=P(None, "seq", "chan"), check_vma=False
    )
```

```python
import functools

import jax
import jax.numpy as jnp
from jax import lax
from jax.experimental import pallas as pl
from jax.experimental.pallas import tpu as pltpu
from jax.sharding import PartitionSpec as P

F32 = jnp.float32
BF16 = jnp.bfloat16
LANES = 128
CH = 8
ROWS = 160
HEAD = 128
TAIL = ROWS - HEAD
FOLD = LANES // TAIL
PER = CH + CH // FOLD
PEERS = 128
MSG = PEERS * PER
VMEM_LIMIT = 48 * 1024 * 1024
SEQ = "seq"
LINE = 8
AWAY = (0, 4, 2, -2, 1, 3, -1, -3)


def full(shape):
    return pl.BlockSpec(shape, lambda: (0,) * len(shape))


def call(kernel, out, ins, scratch, flops=0, smem=0):
    args = ins
    in_specs = [pl.BlockSpec(memory_space=pltpu.SMEM)] * smem
    in_specs += [full(a.shape) for a in args[smem:]]
    nbytes = sum(a.size * a.dtype.itemsize for a in args)
    nbytes += out.size * out.dtype.itemsize
    return pl.pallas_call(
        kernel,
        out_shape=out,
        in_specs=in_specs,
        out_specs=full(out.shape),
        scratch_shapes=scratch,
        compiler_params=pltpu.CompilerParams(vmem_limit_bytes=VMEM_LIMIT),
        cost_estimate=pl.CostEstimate(flops=flops, bytes_accessed=nbytes, transcendentals=0),
    )(*args)


def pack_kernel(v_ref, out_ref, msg, low):
    for j in range(8):
        cols = slice(j * LANES, (j + 1) * LANES)
        block = v_ref[:, cols].astype(F32)
        head = block[:HEAD].T
        for g in range(16):
            msg[pl.ds((16 * j + g) * PER, CH), :] = head[g * CH : (g + 1) * CH]
        low[cols, :TAIL] = block[HEAD:].T
    for i in range(CH // FOLD):
        parts = [low[pl.ds(FOLD * i + k, PEERS, stride=CH), :][:, :TAIL] for k in range(FOLD)]
        msg[pl.ds(CH + i, PEERS, stride=PER), :] = jnp.concatenate(parts, axis=1)
    out_ref[...] = msg[...].astype(BF16)


def toeplitz_kernel(index_ref, f_ref, out_ref, taps):
    group = index_ref[0]
    tile = pl.multiple_of(lax.div(group, 16) * LANES, LANES)
    taps[...] = f_ref[:, pl.ds(tile, LANES)].astype(F32).T
    mine = taps[pl.ds(pl.multiple_of(lax.rem(group, 16) * CH, CH), CH), :]
    row = lax.broadcasted_iota(jnp.int32, (LANES, LANES), 0)
    lane = lax.broadcasted_iota(jnp.int32, (LANES, LANES), 1)
    for c in range(CH):
        spread = jnp.broadcast_to(mine[c : c + 1, :], (LANES, 2 * LANES))
        turned = pltpu.roll(spread, 0, 1, stride=1, stride_axis=0)
        near = jnp.where(lane >= row, turned[:, :LANES], 0.0).astype(BF16)
        out_ref[c, :LANES, :LANES] = near
        out_ref[c, LANES:, LANES:] = near
        out_ref[c, :LANES, LANES:] = turned[:, LANES:].astype(BF16)
        out_ref[c, LANES:, :LANES] = jnp.zeros((LANES, LANES), BF16)


def conv_kernel(start_ref, length_ref, skip_ref, in_ref, toep_ref, out_ref, msg, seq, result, first, second):
    msg[...] = in_ref[...].astype(F32)
    for c in range(CH):
        seq[pl.ds(c, HEAD, stride=CH), :] = msg[pl.ds(c, PEERS, stride=PER), :].T
    for i in range(CH // FOLD):
        tail = msg[pl.ds(CH + i, PEERS, stride=PER), :].T
        for k in range(FOLD):
            seq[pl.ds(HEAD * CH + FOLD * i + k, TAIL, stride=CH), :] = tail[k * TAIL : (k + 1) * TAIL]
    result[...] = jnp.zeros_like(result)
    lane = lax.broadcasted_iota(jnp.int32, (CH, LANES), 1)

    def take(d, carry):
        begin, length = start_ref[d], length_ref[d]
        row = pl.multiple_of(lax.shift_right_logical(begin, 7) * CH, CH)
        turn = begin & (LANES - 1)
        back = (LANES - turn) & (LANES - 1)
        pieces = [pltpu.roll(seq[pl.ds(row + CH * i, CH), :], back, 1) for i in range(3)]
        whole = lane < LANES - turn
        near = jnp.where(whole, pieces[0], pieces[1])
        far = jnp.where(whole, pieces[1], pieces[2])
        first[pl.ds(d, CH, stride=PEERS), :] = jnp.where(lane < length, near, 0.0)
        second[pl.ds(d, CH, stride=PEERS), :] = jnp.where(lane < length - LANES, far, 0.0)
        return carry

    lax.fori_loop(0, PEERS, take, 0, unroll=8)
    for c in range(CH):
        rows = slice(c * PEERS, (c + 1) * PEERS)
        near, far = first[rows, :], second[rows, :]
        both = jnp.concatenate([near, far], axis=1).astype(BF16)
        done = jnp.dot(both, toep_ref[c], preferred_element_type=F32)
        gain = skip_ref[c]
        first[rows, :] = (done[:, :LANES] + gain * near).astype(BF16).astype(F32)
        second[rows, :] = (done[:, LANES:] + gain * far).astype(BF16).astype(F32)

    def give(d, carry):
        begin, length = start_ref[d], length_ref[d]
        row = pl.multiple_of(lax.shift_right_logical(begin, 7) * CH, CH)
        turn = begin & (LANES - 1)
        near = jnp.where(lane < length, first[pl.ds(d, CH, stride=PEERS), :], 0.0)
        far = jnp.where(lane < length - LANES, second[pl.ds(d, CH, stride=PEERS), :], 0.0)
        near = pltpu.roll(near, turn, 1)
        far = pltpu.roll(far, turn, 1)
        whole = lane >= turn
        result[pl.ds(row, CH), :] += jnp.where(whole, near, 0.0)
        result[pl.ds(row + CH, CH), :] += jnp.where(whole, far, near)
        result[pl.ds(row + 2 * CH, CH), :] += jnp.where(whole, 0.0, far)
        return carry

    lax.fori_loop(0, PEERS, give, 0, unroll=8)
    for c in range(CH):
        msg[pl.ds(c, PEERS, stride=PER), :] = result[pl.ds(c, HEAD, stride=CH), :].T
    for i in range(CH // FOLD):
        parts = [result[pl.ds(HEAD * CH + FOLD * i + k, TAIL, stride=CH), :] for k in range(FOLD)]
        msg[pl.ds(CH + i, PEERS, stride=PER), :] = jnp.concatenate(parts, axis=0).T
    out_ref[...] = msg[...].astype(BF16)


def gate_kernel(in_ref, g_ref, out_ref, msg, low):
    msg[...] = in_ref[...].astype(F32)
    for i in range(CH // FOLD):
        tail = msg[pl.ds(CH + i, PEERS, stride=PER), :]
        for k in range(FOLD):
            low[pl.ds(FOLD * i + k, PEERS, stride=CH), :TAIL] = tail[:, k * TAIL : (k + 1) * TAIL]
    for j in range(8):
        cols = slice(j * LANES, (j + 1) * LANES)
        head = [msg[pl.ds((16 * j + g) * PER, CH), :] for g in range(16)]
        head = jnp.concatenate(head, axis=0).T
        head = (head * g_ref[:HEAD, cols].astype(F32)).astype(BF16)
        tail = low[cols, :].T[:TAIL]
        tail = (tail * g_ref[HEAD:, cols].astype(F32)).astype(BF16)
        for q in range(out_ref.shape[0]):
            out_ref[q, :HEAD, cols] = head
            out_ref[q, HEAD:, cols] = tail


def multiply(rows_ref, w_ref):
    groups, _, width = rows_ref.shape
    total = jnp.zeros((w_ref.shape[0], ROWS), F32)
    for q in range(groups):
        part = w_ref[:, q * width : (q + 1) * width]
        total += lax.dot_general(part, rows_ref[q], (((1,), (1,)), ((), ())), preferred_element_type=F32)
    return total


def own_kernel(rows_ref, near_ref, far_ref, out_ref):
    half = near_ref.shape[0]
    out_ref[:half] = multiply(rows_ref, near_ref)
    out_ref[half:] = multiply(rows_ref, far_ref)


def other_kernel(index_ref, rows_ref, near_ref, far_ref, own_ref, out_ref, other, columns):
    half = near_ref.shape[0]
    other[:half] = multiply(rows_ref, near_ref)
    other[half:] = multiply(rows_ref, far_ref)
    index = index_ref[0]
    z, y, core = lax.shift_right_logical(index, 4), lax.shift_right_logical(index, 1) & 7, index & 1
    for source, origin in ((own_ref, core), (other, 1 - core)):
        straight = origin == 0
        outer, outer_step = jnp.where(straight, z, y), jnp.where(straight, 16, 2)
        inner, inner_step = jnp.where(straight, y, z), jnp.where(straight, 2, 16)
        inners = [((inner + AWAY[a]) & 7) * inner_step + origin for a in range(LINE)]
        for b in range(LINE):
            base = ((outer + AWAY[b]) & 7) * outer_step
            for a in range(LINE):
                group = base + inners[a]
                rows = slice((LINE * b + a) * CH, (LINE * b + a + 1) * CH)
                columns[pl.ds(pl.multiple_of(group * CH, CH), CH), :] = source[rows, :]
    for j in range(8):
        cols = slice(j * LANES, (j + 1) * LANES)
        out_ref[:, cols] = columns[cols, :].T.astype(BF16)


def exchange(message):
    sent = message.reshape(PEERS, PER // 2, 2, LANES)
    got = lax.all_to_all(sent, SEQ, split_axis=0, concat_axis=0, tiled=True)
    return got.reshape(MSG, LANES)


def local(values, gates, filters, skip, weights, doc_lengths):
    index = lax.axis_index(SEQ).astype(jnp.int32)
    width = values.shape[2]
    msg = jax.ShapeDtypeStruct((MSG, LANES), BF16)
    buf = pltpu.VMEM((MSG, LANES), F32)
    low = pltpu.VMEM((width, LANES), F32)
    packed = call(pack_kernel, msg, [values.reshape(ROWS, width)], [buf, low])
    packed, filters, doc_lengths, skip, shard = lax.optimization_barrier(
        (packed, filters, doc_lengths, skip, weights.T)
    )
    line = first_line(shard)
    toep = call(
        toeplitz_kernel,
        jax.ShapeDtypeStruct((CH, 2 * LANES, 2 * LANES), BF16),
        [index[None], filters],
        [pltpu.VMEM((LANES, 2 * LANES), F32)],
        smem=1,
    )
    starts = jnp.cumsum(doc_lengths) - doc_lengths
    own_skip = lax.dynamic_slice(skip, (index * CH,), (CH,))
    got = exchange(packed)
    line, toep, starts, own_skip = lax.optimization_barrier((line, toep, starts, own_skip))
    fars = direct(line, "z")
    convolved = call(
        conv_kernel,
        msg,
        [starts, doc_lengths, own_skip, got, toep],
        [
            buf,
            pltpu.VMEM((MSG + 3 * CH, LANES), F32),
            pltpu.VMEM((MSG + 3 * CH, LANES), F32),
            pltpu.VMEM((CH * PEERS, LANES), F32),
            pltpu.VMEM((CH * PEERS, LANES), F32),
        ],
        flops=2 * CH * PEERS * 256 * 256,
        smem=3,
    )
    block, four, two, back_two, _ = lax.optimization_barrier((line, *fars, convolved))
    near = jnp.concatenate([block, four, two, back_two], axis=0)
    back, *sides = lax.optimization_barrier((exchange(convolved), *handed(block, two, back_two, "z")))
    own = near, jnp.concatenate(sides, axis=0)
    other = tuple(lax.ppermute(part, "seq", [(i, i ^ 1) for i in range(PEERS)]) for part in own)
    groups = lax.axis_size("chan")
    copies = call(
        gate_kernel,
        jax.ShapeDtypeStruct((groups, ROWS, width), BF16),
        [back, gates.reshape(ROWS, width)],
        [buf, low],
    )
    rows = lax.all_to_all(copies, "chan", split_axis=0, concat_axis=0, tiled=True)
    wide = own[0].shape[0] + own[1].shape[0]
    half = jax.ShapeDtypeStruct((wide, ROWS), F32)
    flops = 2 * ROWS * wide * own[0].shape[1]
    first = call(own_kernel, half, [rows, *own], [], flops=flops)
    mixed = call(
        other_kernel,
        jax.ShapeDtypeStruct((ROWS, width), BF16),
        [index[None], rows, *other, first],
        [pltpu.VMEM((wide, ROWS), F32), pltpu.VMEM((2 * wide, ROWS), F32)],
        flops=flops,
        smem=1,
    )
    return mixed[:, None, :]


def lines(first):
    along = {"y": [], "z": []}
    for core in range(2):
        axis = first if core == 0 else ("z" if first == "y" else "y")
        for fixed in range(8):
            along[axis].append([(fixed * 16 + i * 2 if axis == "y" else i * 16 + fixed * 2) + core for i in range(8)])
    return along["y"] + along["z"]


def move(array, first, places):
    pairs = [(line[(i + places) % LINE], line[i]) for line in lines(first) for i in range(LINE)]
    return lax.ppermute(array, "seq", pairs)


def direct(block, first):
    return tuple(move(block, first, places) for places in AWAY[1:4])


def handed(block, two, back_two, first):
    one = move(jnp.concatenate([block, two], axis=0), first, 1)
    return one, move(jnp.concatenate([block, back_two], axis=0), first, -1)


def first_line(shard):
    four, two, back_two = direct(shard, "y")
    return jnp.concatenate([shard, four, two, back_two, *handed(shard, two, back_two, "y")], axis=0)


def solution(mesh):
    placed = (
        P(None, "seq", "chan"),
        P(None, "seq", "chan"),
        P(None, "chan"),
        P("chan"),
        P(None, ("chan", "seq")),
        P(),
    )
    return jax.shard_map(
        local, mesh=mesh, in_specs=placed, out_specs=P(None, "seq", "chan"), check_vma=False
    )
```

```python
import functools

import jax
import jax.numpy as jnp
from jax import lax
from jax.experimental import pallas as pl
from jax.experimental.pallas import tpu as pltpu
from jax.sharding import PartitionSpec as P

F32 = jnp.float32
BF16 = jnp.bfloat16
LANES = 128
CH = 8
ROWS = 160
HEAD = 128
TAIL = ROWS - HEAD
FOLD = LANES // TAIL
PER = CH + CH // FOLD
PEERS = 128
MSG = PEERS * PER
VMEM_LIMIT = 48 * 1024 * 1024
SEQ = "seq"


def full(shape):
    return pl.BlockSpec(shape, lambda: (0,) * len(shape))


def call(kernel, out, ins, scratch, flops=0, smem=0):
    args = ins
    in_specs = [pl.BlockSpec(memory_space=pltpu.SMEM)] * smem
    in_specs += [full(a.shape) for a in args[smem:]]
    nbytes = sum(a.size * a.dtype.itemsize for a in args)
    nbytes += out.size * out.dtype.itemsize
    return pl.pallas_call(
        kernel,
        out_shape=out,
        in_specs=in_specs,
        out_specs=full(out.shape),
        scratch_shapes=scratch,
        compiler_params=pltpu.CompilerParams(vmem_limit_bytes=VMEM_LIMIT),
        cost_estimate=pl.CostEstimate(flops=flops, bytes_accessed=nbytes, transcendentals=0),
    )(*args)


def pack_kernel(v_ref, out_ref, msg, low):
    for j in range(8):
        cols = slice(j * LANES, (j + 1) * LANES)
        block = v_ref[:, cols].astype(F32)
        head = block[:HEAD].T
        for g in range(16):
            msg[pl.ds((16 * j + g) * PER, CH), :] = head[g * CH : (g + 1) * CH]
        low[cols, :TAIL] = block[HEAD:].T
    for i in range(CH // FOLD):
        parts = [low[pl.ds(FOLD * i + k, PEERS, stride=CH), :][:, :TAIL] for k in range(FOLD)]
        msg[pl.ds(CH + i, PEERS, stride=PER), :] = jnp.concatenate(parts, axis=1)
    out_ref[...] = msg[...].astype(BF16)


def toeplitz_kernel(index_ref, f_ref, out_ref, taps):
    group = index_ref[0]
    tile = pl.multiple_of(lax.div(group, 16) * LANES, LANES)
    taps[...] = f_ref[:, pl.ds(tile, LANES)].astype(F32).T
    mine = taps[pl.ds(pl.multiple_of(lax.rem(group, 16) * CH, CH), CH), :]
    row = lax.broadcasted_iota(jnp.int32, (LANES, LANES), 0)
    lane = lax.broadcasted_iota(jnp.int32, (LANES, LANES), 1)
    for c in range(CH):
        spread = jnp.broadcast_to(mine[c : c + 1, :], (LANES, 2 * LANES))
        turned = pltpu.roll(spread, 0, 1, stride=1, stride_axis=0)
        near = jnp.where(lane >= row, turned[:, :LANES], 0.0).astype(BF16)
        out_ref[c, :LANES, :LANES] = near
        out_ref[c, LANES:, LANES:] = near
        out_ref[c, :LANES, LANES:] = turned[:, LANES:].astype(BF16)
        out_ref[c, LANES:, :LANES] = jnp.zeros((LANES, LANES), BF16)


def conv_kernel(start_ref, length_ref, skip_ref, in_ref, toep_ref, out_ref, msg, seq, result, first, second):
    msg[...] = in_ref[...].astype(F32)
    for c in range(CH):
        seq[pl.ds(c, HEAD, stride=CH), :] = msg[pl.ds(c, PEERS, stride=PER), :].T
    for i in range(CH // FOLD):
        tail = msg[pl.ds(CH + i, PEERS, stride=PER), :].T
        for k in range(FOLD):
            seq[pl.ds(HEAD * CH + FOLD * i + k, TAIL, stride=CH), :] = tail[k * TAIL : (k + 1) * TAIL]
    result[...] = jnp.zeros_like(result)
    lane = lax.broadcasted_iota(jnp.int32, (CH, LANES), 1)

    def take(d, carry):
        begin, length = start_ref[d], length_ref[d]
        row = pl.multiple_of(lax.shift_right_logical(begin, 7) * CH, CH)
        turn = begin & (LANES - 1)
        back = (LANES - turn) & (LANES - 1)
        pieces = [pltpu.roll(seq[pl.ds(row + CH * i, CH), :], back, 1) for i in range(3)]
        whole = lane < LANES - turn
        near = jnp.where(whole, pieces[0], pieces[1])
        far = jnp.where(whole, pieces[1], pieces[2])
        first[pl.ds(d, CH, stride=PEERS), :] = jnp.where(lane < length, near, 0.0)
        second[pl.ds(d, CH, stride=PEERS), :] = jnp.where(lane < length - LANES, far, 0.0)
        return carry

    lax.fori_loop(0, PEERS, take, 0, unroll=8)
    for c in range(CH):
        rows = slice(c * PEERS, (c + 1) * PEERS)
        near, far = first[rows, :], second[rows, :]
        both = jnp.concatenate([near, far], axis=1).astype(BF16)
        done = jnp.dot(both, toep_ref[c], preferred_element_type=F32)
        gain = skip_ref[c]
        first[rows, :] = (done[:, :LANES] + gain * near).astype(BF16).astype(F32)
        second[rows, :] = (done[:, LANES:] + gain * far).astype(BF16).astype(F32)

    def give(d, carry):
        begin, length = start_ref[d], length_ref[d]
        row = pl.multiple_of(lax.shift_right_logical(begin, 7) * CH, CH)
        turn = begin & (LANES - 1)
        near = jnp.where(lane < length, first[pl.ds(d, CH, stride=PEERS), :], 0.0)
        far = jnp.where(lane < length - LANES, second[pl.ds(d, CH, stride=PEERS), :], 0.0)
        near = pltpu.roll(near, turn, 1)
        far = pltpu.roll(far, turn, 1)
        whole = lane >= turn
        result[pl.ds(row, CH), :] += jnp.where(whole, near, 0.0)
        result[pl.ds(row + CH, CH), :] += jnp.where(whole, far, near)
        result[pl.ds(row + 2 * CH, CH), :] += jnp.where(whole, 0.0, far)
        return carry

    lax.fori_loop(0, PEERS, give, 0, unroll=8)
    for c in range(CH):
        msg[pl.ds(c, PEERS, stride=PER), :] = result[pl.ds(c, HEAD, stride=CH), :].T
    for i in range(CH // FOLD):
        parts = [result[pl.ds(HEAD * CH + FOLD * i + k, TAIL, stride=CH), :] for k in range(FOLD)]
        msg[pl.ds(CH + i, PEERS, stride=PER), :] = jnp.concatenate(parts, axis=0).T
    out_ref[...] = msg[...].astype(BF16)


def gate_kernel(in_ref, g_ref, out_ref, msg, low):
    msg[...] = in_ref[...].astype(F32)
    for i in range(CH // FOLD):
        tail = msg[pl.ds(CH + i, PEERS, stride=PER), :]
        for k in range(FOLD):
            low[pl.ds(FOLD * i + k, PEERS, stride=CH), :TAIL] = tail[:, k * TAIL : (k + 1) * TAIL]
    for j in range(8):
        cols = slice(j * LANES, (j + 1) * LANES)
        head = [msg[pl.ds((16 * j + g) * PER, CH), :] for g in range(16)]
        head = jnp.concatenate(head, axis=0).T
        head = (head * g_ref[:HEAD, cols].astype(F32)).astype(BF16)
        tail = low[cols, :].T[:TAIL]
        tail = (tail * g_ref[HEAD:, cols].astype(F32)).astype(BF16)
        for q in range(out_ref.shape[0]):
            out_ref[q, :HEAD, cols] = head
            out_ref[q, HEAD:, cols] = tail


def multiply(rows_ref, w_ref):
    groups, _, width = rows_ref.shape
    total = jnp.zeros((w_ref.shape[0], ROWS), F32)
    for q in range(groups):
        part = w_ref[:, q * width : (q + 1) * width]
        total += lax.dot_general(part, rows_ref[q], (((1,), (1,)), ((), ())), preferred_element_type=F32)
    return total


def product_kernel(rows_ref, w_ref, out_ref):
    out_ref[...] = multiply(rows_ref, w_ref).astype(out_ref.dtype)


def join_kernel(core_ref, own_ref, other_ref, out_ref, zy, yz):
    other = other_ref[...].astype(F32)
    own_first = core_ref[0] == 0
    own = own_ref[...]
    zy[...] = jnp.where(own_first, own, other)
    yz[...] = jnp.where(own_first, other, own)
    for z in range(8):
        parts = []
        for y in range(8):
            parts.append(zy[(8 * z + y) * 8 : (8 * z + y + 1) * 8, :])
            parts.append(yz[(8 * y + z) * 8 : (8 * y + z + 1) * 8, :])
        block = jnp.concatenate(parts, axis=0)
        out_ref[:, z * LANES : (z + 1) * LANES] = block.T.astype(BF16)


def exchange(message):
    sent = message.reshape(PEERS, PER // 2, 2, LANES)
    got = lax.all_to_all(sent, SEQ, split_axis=0, concat_axis=0, tiled=True)
    return got.reshape(MSG, LANES)


def local(values, gates, filters, skip, weights, doc_lengths):
    index = lax.axis_index(SEQ).astype(jnp.int32)
    width = values.shape[2]
    msg = jax.ShapeDtypeStruct((MSG, LANES), BF16)
    buf = pltpu.VMEM((MSG, LANES), F32)
    low = pltpu.VMEM((width, LANES), F32)
    packed = call(pack_kernel, msg, [values.reshape(ROWS, width)], [buf, low])
    packed, filters, doc_lengths, skip, shard = lax.optimization_barrier(
        (packed, filters, doc_lengths, skip, weights.T)
    )
    line = gather_line(shard)
    toep = call(
        toeplitz_kernel,
        jax.ShapeDtypeStruct((CH, 2 * LANES, 2 * LANES), BF16),
        [index[None], filters],
        [pltpu.VMEM((LANES, 2 * LANES), F32)],
        smem=1,
    )
    starts = jnp.cumsum(doc_lengths) - doc_lengths
    own_skip = lax.dynamic_slice(skip, (index * CH,), (CH,))
    got, line, toep, starts, own_skip = lax.optimization_barrier(
        (exchange(packed), line, toep, starts, own_skip)
    )
    own = lax.all_gather(line, "seq", axis=0, axis_index_groups=lines("z"), tiled=True)
    convolved = call(
        conv_kernel,
        msg,
        [starts, doc_lengths, own_skip, got, toep],
        [
            buf,
            pltpu.VMEM((MSG + 3 * CH, LANES), F32),
            pltpu.VMEM((MSG + 3 * CH, LANES), F32),
            pltpu.VMEM((CH * PEERS, LANES), F32),
            pltpu.VMEM((CH * PEERS, LANES), F32),
        ],
        flops=2 * CH * PEERS * 256 * 256,
        smem=3,
    )
    back = exchange(convolved)
    groups = lax.axis_size("chan")
    copies = call(
        gate_kernel,
        jax.ShapeDtypeStruct((groups, ROWS, width), BF16),
        [back, gates.reshape(ROWS, width)],
        [buf, low],
    )
    rows = lax.all_to_all(copies, "chan", split_axis=0, concat_axis=0, tiled=True)
    swap = [(i, i ^ 1) for i in range(PEERS)]
    half = (own.shape[0], ROWS)
    flops = 2 * ROWS * own.size
    twin_rows = lax.ppermute(rows, "seq", swap)
    mine = call(product_kernel, jax.ShapeDtypeStruct(half, F32), [rows, own], [], flops=flops)
    theirs = call(product_kernel, jax.ShapeDtypeStruct(half, BF16), [twin_rows, own], [], flops=flops)
    mixed = call(
        join_kernel,
        jax.ShapeDtypeStruct((ROWS, width), BF16),
        [lax.rem(index, 2)[None], mine, lax.ppermute(theirs, "seq", swap)],
        [pltpu.VMEM(half, F32)] * 2,
        smem=1,
    )
    return mixed[:, None, :]


def lines(first):
    along = {"y": [], "z": []}
    for core in range(2):
        axis = first if core == 0 else ("z" if first == "y" else "y")
        for fixed in range(8):
            along[axis].append([(fixed * 16 + i * 2 if axis == "y" else i * 16 + fixed * 2) + core for i in range(8)])
    return along["y"] + along["z"]


def gather_line(shard):
    return lax.all_gather(shard, "seq", axis=0, axis_index_groups=lines("y"), tiled=True)


def solution(mesh):
    placed = (
        P(None, "seq", "chan"),
        P(None, "seq", "chan"),
        P(None, "chan"),
        P("chan"),
        P(None, ("chan", "seq")),
        P(),
    )
    return jax.shard_map(
        local, mesh=mesh, in_specs=placed, out_specs=P(None, "seq", "chan"), check_vma=False
    )
```

```python
import functools

import jax
import jax.numpy as jnp
from jax import lax
from jax.experimental import pallas as pl
from jax.experimental.pallas import tpu as pltpu
from jax.sharding import Mesh
from jax.sharding import PartitionSpec as P

F32 = jnp.float32
BF16 = jnp.bfloat16
LANES = 128
CH = 8
ROWS = 160
HEAD = 128
TAIL = ROWS - HEAD
FOLD = LANES // TAIL
PER = CH + CH // FOLD
PEERS = 128
MSG = PEERS * PER
VMEM_LIMIT = 48 * 1024 * 1024
SEQ = ("z", "y_far", "y_near", "core")
NEAR = 1


def full(shape):
    return pl.BlockSpec(shape, lambda: (0,) * len(shape))


def call(kernel, out, ins, scratch, flops=0, smem=0):
    args = ins
    in_specs = [pl.BlockSpec(memory_space=pltpu.SMEM)] * smem
    in_specs += [full(a.shape) for a in args[smem:]]
    nbytes = sum(a.size * a.dtype.itemsize for a in args)
    nbytes += out.size * out.dtype.itemsize
    return pl.pallas_call(
        kernel,
        out_shape=out,
        in_specs=in_specs,
        out_specs=full(out.shape),
        scratch_shapes=scratch,
        compiler_params=pltpu.CompilerParams(vmem_limit_bytes=VMEM_LIMIT),
        cost_estimate=pl.CostEstimate(flops=flops, bytes_accessed=nbytes, transcendentals=0),
    )(*args)


def pack_kernel(v_ref, out_ref, msg, low):
    for j in range(8):
        cols = slice(j * LANES, (j + 1) * LANES)
        block = v_ref[:, cols].astype(F32)
        head = block[:HEAD].T
        for g in range(16):
            msg[pl.ds((16 * j + g) * PER, CH), :] = head[g * CH : (g + 1) * CH]
        low[cols, :TAIL] = block[HEAD:].T
    for i in range(CH // FOLD):
        parts = [low[pl.ds(FOLD * i + k, PEERS, stride=CH), :][:, :TAIL] for k in range(FOLD)]
        msg[pl.ds(CH + i, PEERS, stride=PER), :] = jnp.concatenate(parts, axis=1)
    out_ref[...] = msg[...].astype(BF16)


def toeplitz_kernel(index_ref, f_ref, out_ref, taps):
    group = index_ref[0]
    tile = pl.multiple_of(lax.div(group, 16) * LANES, LANES)
    taps[...] = f_ref[:, pl.ds(tile, LANES)].astype(F32).T
    mine = taps[pl.ds(pl.multiple_of(lax.rem(group, 16) * CH, CH), CH), :]
    row = lax.broadcasted_iota(jnp.int32, (LANES, LANES), 0)
    lane = lax.broadcasted_iota(jnp.int32, (LANES, LANES), 1)
    for c in range(CH):
        spread = jnp.broadcast_to(mine[c : c + 1, :], (LANES, 2 * LANES))
        turned = pltpu.roll(spread, 0, 1, stride=1, stride_axis=0)
        near = jnp.where(lane >= row, turned[:, :LANES], 0.0).astype(BF16)
        out_ref[c, :LANES, :LANES] = near
        out_ref[c, LANES:, LANES:] = near
        out_ref[c, :LANES, LANES:] = turned[:, LANES:].astype(BF16)
        out_ref[c, LANES:, :LANES] = jnp.zeros((LANES, LANES), BF16)


def conv_kernel(start_ref, length_ref, skip_ref, in_ref, toep_ref, out_ref, msg, seq, result, first, second):
    msg[...] = in_ref[...].astype(F32)
    for c in range(CH):
        seq[pl.ds(c, HEAD, stride=CH), :] = msg[pl.ds(c, PEERS, stride=PER), :].T
    for i in range(CH // FOLD):
        tail = msg[pl.ds(CH + i, PEERS, stride=PER), :].T
        for k in range(FOLD):
            seq[pl.ds(HEAD * CH + FOLD * i + k, TAIL, stride=CH), :] = tail[k * TAIL : (k + 1) * TAIL]
    result[...] = jnp.zeros_like(result)
    lane = lax.broadcasted_iota(jnp.int32, (CH, LANES), 1)

    def take(d, carry):
        begin, length = start_ref[d], length_ref[d]
        row = pl.multiple_of(lax.shift_right_logical(begin, 7) * CH, CH)
        turn = begin & (LANES - 1)
        back = (LANES - turn) & (LANES - 1)
        pieces = [pltpu.roll(seq[pl.ds(row + CH * i, CH), :], back, 1) for i in range(3)]
        whole = lane < LANES - turn
        near = jnp.where(whole, pieces[0], pieces[1])
        far = jnp.where(whole, pieces[1], pieces[2])
        first[pl.ds(d, CH, stride=PEERS), :] = jnp.where(lane < length, near, 0.0)
        second[pl.ds(d, CH, stride=PEERS), :] = jnp.where(lane < length - LANES, far, 0.0)
        return carry

    lax.fori_loop(0, PEERS, take, 0, unroll=8)
    for c in range(CH):
        rows = slice(c * PEERS, (c + 1) * PEERS)
        near, far = first[rows, :], second[rows, :]
        both = jnp.concatenate([near, far], axis=1).astype(BF16)
        done = jnp.dot(both, toep_ref[c], preferred_element_type=F32)
        gain = skip_ref[c]
        first[rows, :] = (done[:, :LANES] + gain * near).astype(BF16).astype(F32)
        second[rows, :] = (done[:, LANES:] + gain * far).astype(BF16).astype(F32)

    def give(d, carry):
        begin, length = start_ref[d], length_ref[d]
        row = pl.multiple_of(lax.shift_right_logical(begin, 7) * CH, CH)
        turn = begin & (LANES - 1)
        near = jnp.where(lane < length, first[pl.ds(d, CH, stride=PEERS), :], 0.0)
        far = jnp.where(lane < length - LANES, second[pl.ds(d, CH, stride=PEERS), :], 0.0)
        near = pltpu.roll(near, turn, 1)
        far = pltpu.roll(far, turn, 1)
        whole = lane >= turn
        result[pl.ds(row, CH), :] += jnp.where(whole, near, 0.0)
        result[pl.ds(row + CH, CH), :] += jnp.where(whole, far, near)
        result[pl.ds(row + 2 * CH, CH), :] += jnp.where(whole, 0.0, far)
        return carry

    lax.fori_loop(0, PEERS, give, 0, unroll=8)
    for c in range(CH):
        msg[pl.ds(c, PEERS, stride=PER), :] = result[pl.ds(c, HEAD, stride=CH), :].T
    for i in range(CH // FOLD):
        parts = [result[pl.ds(HEAD * CH + FOLD * i + k, TAIL, stride=CH), :] for k in range(FOLD)]
        msg[pl.ds(CH + i, PEERS, stride=PER), :] = jnp.concatenate(parts, axis=0).T
    out_ref[...] = msg[...].astype(BF16)


def gate_kernel(in_ref, g_ref, out_ref, msg, low):
    msg[...] = in_ref[...].astype(F32)
    for i in range(CH // FOLD):
        tail = msg[pl.ds(CH + i, PEERS, stride=PER), :]
        for k in range(FOLD):
            low[pl.ds(FOLD * i + k, PEERS, stride=CH), :TAIL] = tail[:, k * TAIL : (k + 1) * TAIL]
    for j in range(8):
        cols = slice(j * LANES, (j + 1) * LANES)
        head = [msg[pl.ds((16 * j + g) * PER, CH), :] for g in range(16)]
        head = jnp.concatenate(head, axis=0).T
        head = (head * g_ref[:HEAD, cols].astype(F32)).astype(BF16)
        tail = low[cols, :].T[:TAIL]
        tail = (tail * g_ref[HEAD:, cols].astype(F32)).astype(BF16)
        for q in range(out_ref.shape[0]):
            out_ref[q, :HEAD, cols] = head
            out_ref[q, HEAD:, cols] = tail


def product_kernel(near, rows_ref, w_ref, out_ref):
    groups, _, width = rows_ref.shape
    total = jnp.zeros((w_ref.shape[0], ROWS), F32)
    for q in range(groups):
        part = w_ref[:, q * width : (q + 1) * width]
        total += lax.dot_general(part, rows_ref[q], (((1,), (1,)), ((), ())), preferred_element_type=F32)
    for j in range(w_ref.shape[0] // LANES):
        parts = []
        for y in range(8):
            for core in range(2):
                group = 16 * j + y // near * 2 * near + core * near + y % near
                parts.append(total[group * CH : (group + 1) * CH])
        block = jnp.concatenate(parts, axis=0)
        out_ref[:, j * LANES : (j + 1) * LANES] = block.T.astype(BF16)


def product(rows, table, near):
    block = 256
    return pl.pallas_call(
        functools.partial(product_kernel, near),
        out_shape=jax.ShapeDtypeStruct((ROWS, table.shape[0]), BF16),
        grid=(table.shape[0] // block,),
        in_specs=[
            pl.BlockSpec(rows.shape, lambda j: (0, 0, 0)),
            pl.BlockSpec((block, table.shape[1]), lambda j: (j, 0)),
        ],
        out_specs=pl.BlockSpec((ROWS, block), lambda j: (0, j)),
        compiler_params=pltpu.CompilerParams(vmem_limit_bytes=VMEM_LIMIT),
        cost_estimate=pl.CostEstimate(
            flops=2 * ROWS * table.size,
            bytes_accessed=2 * (table.size + rows.size + ROWS * table.shape[0]),
            transcendentals=0,
        ),
    )(rows, table)


def exchange(message):
    sent = message.reshape(PEERS, PER // 2, 2, LANES)
    got = lax.all_to_all(sent, SEQ, split_axis=0, concat_axis=0, tiled=True)
    return got.reshape(MSG, LANES)


def local(values, gates, filters, skip, weights, doc_lengths):
    index = lax.axis_index(SEQ).astype(jnp.int32)
    width = values.shape[2]
    msg = jax.ShapeDtypeStruct((MSG, LANES), BF16)
    buf = pltpu.VMEM((MSG, LANES), F32)
    low = pltpu.VMEM((width, LANES), F32)
    packed = call(pack_kernel, msg, [values.reshape(ROWS, width)], [buf, low])
    table = gather_columns(weights.T)
    packed, filters, doc_lengths, skip = lax.optimization_barrier((packed, filters, doc_lengths, skip))
    toep = call(
        toeplitz_kernel,
        jax.ShapeDtypeStruct((CH, 2 * LANES, 2 * LANES), BF16),
        [index[None], filters],
        [pltpu.VMEM((LANES, 2 * LANES), F32)],
        smem=1,
    )
    starts = jnp.cumsum(doc_lengths) - doc_lengths
    own_skip = lax.dynamic_slice(skip, (index * CH,), (CH,))
    got, toep, starts, own_skip = lax.optimization_barrier((exchange(packed), toep, starts, own_skip))
    convolved = call(
        conv_kernel,
        msg,
        [starts, doc_lengths, own_skip, got, toep],
        [
            buf,
            pltpu.VMEM((MSG + 3 * CH, LANES), F32),
            pltpu.VMEM((MSG + 3 * CH, LANES), F32),
            pltpu.VMEM((CH * PEERS, LANES), F32),
            pltpu.VMEM((CH * PEERS, LANES), F32),
        ],
        flops=2 * CH * PEERS * 256 * 256,
        smem=3,
    )
    back = exchange(convolved)
    groups = lax.axis_size("chan")
    copies = call(
        gate_kernel,
        jax.ShapeDtypeStruct((groups, ROWS, width), BF16),
        [back, gates.reshape(ROWS, width)],
        [buf, low],
    )
    rows = lax.all_to_all(copies, "chan", split_axis=0, concat_axis=0, tiled=True)
    mixed = product(rows, table, NEAR)
    return mixed[:, None, :]


def gather_columns(shard):
    return lax.all_gather(shard, ("z", "y_far", "core"), axis=0, tiled=True)


def solution(mesh):
    shape = dict(z=8, y_far=8 // NEAR, y_near=NEAR, core=2, chan=4)
    fine = Mesh(mesh.devices.reshape(tuple(shape.values())), tuple(shape))
    placed = (
        P(None, SEQ, "chan"),
        P(None, SEQ, "chan"),
        P(None, "chan"),
        P("chan"),
        P(None, ("chan",) + SEQ),
        P(),
    )
    return jax.shard_map(
        local, mesh=fine, in_specs=placed, out_specs=P(None, SEQ, "chan"), check_vma=False
    )
```

```python
import functools

import jax
import jax.numpy as jnp
from jax import lax
from jax.experimental import pallas as pl
from jax.experimental.pallas import tpu as pltpu
from jax.sharding import Mesh
from jax.sharding import PartitionSpec as P

F32 = jnp.float32
BF16 = jnp.bfloat16
LANES = 128
CH = 8
ROWS = 160
HEAD = 128
TAIL = ROWS - HEAD
FOLD = LANES // TAIL
PER = CH + CH // FOLD
PEERS = 128
MSG = PEERS * PER
VMEM_LIMIT = 48 * 1024 * 1024
SEQ = ("z", "y_far", "y_near", "core")
NEAR = 4


def full(shape):
    return pl.BlockSpec(shape, lambda: (0,) * len(shape))


def call(kernel, out, ins, scratch, flops=0, smem=0):
    args = ins
    in_specs = [pl.BlockSpec(memory_space=pltpu.SMEM)] * smem
    in_specs += [full(a.shape) for a in args[smem:]]
    nbytes = sum(a.size * a.dtype.itemsize for a in args)
    nbytes += out.size * out.dtype.itemsize
    return pl.pallas_call(
        kernel,
        out_shape=out,
        in_specs=in_specs,
        out_specs=full(out.shape),
        scratch_shapes=scratch,
        compiler_params=pltpu.CompilerParams(vmem_limit_bytes=VMEM_LIMIT),
        cost_estimate=pl.CostEstimate(flops=flops, bytes_accessed=nbytes, transcendentals=0),
    )(*args)


def pack_kernel(v_ref, out_ref, msg, low):
    for j in range(8):
        cols = slice(j * LANES, (j + 1) * LANES)
        block = v_ref[:, cols].astype(F32)
        head = block[:HEAD].T
        for g in range(16):
            msg[pl.ds((16 * j + g) * PER, CH), :] = head[g * CH : (g + 1) * CH]
        low[cols, :TAIL] = block[HEAD:].T
    for i in range(CH // FOLD):
        parts = [low[pl.ds(FOLD * i + k, PEERS, stride=CH), :][:, :TAIL] for k in range(FOLD)]
        msg[pl.ds(CH + i, PEERS, stride=PER), :] = jnp.concatenate(parts, axis=1)
    out_ref[...] = msg[...].astype(BF16)


def toeplitz_kernel(index_ref, f_ref, out_ref, taps):
    group = index_ref[0]
    tile = pl.multiple_of(lax.div(group, 16) * LANES, LANES)
    taps[...] = f_ref[:, pl.ds(tile, LANES)].astype(F32).T
    mine = taps[pl.ds(pl.multiple_of(lax.rem(group, 16) * CH, CH), CH), :]
    row = lax.broadcasted_iota(jnp.int32, (LANES, LANES), 0)
    lane = lax.broadcasted_iota(jnp.int32, (LANES, LANES), 1)
    for c in range(CH):
        spread = jnp.broadcast_to(mine[c : c + 1, :], (LANES, 2 * LANES))
        turned = pltpu.roll(spread, 0, 1, stride=1, stride_axis=0)
        near = jnp.where(lane >= row, turned[:, :LANES], 0.0).astype(BF16)
        out_ref[c, :LANES, :LANES] = near
        out_ref[c, LANES:, LANES:] = near
        out_ref[c, :LANES, LANES:] = turned[:, LANES:].astype(BF16)
        out_ref[c, LANES:, :LANES] = jnp.zeros((LANES, LANES), BF16)


def conv_kernel(start_ref, length_ref, skip_ref, in_ref, toep_ref, out_ref, msg, seq, result, first, second):
    msg[...] = in_ref[...].astype(F32)
    for c in range(CH):
        seq[pl.ds(c, HEAD, stride=CH), :] = msg[pl.ds(c, PEERS, stride=PER), :].T
    for i in range(CH // FOLD):
        tail = msg[pl.ds(CH + i, PEERS, stride=PER), :].T
        for k in range(FOLD):
            seq[pl.ds(HEAD * CH + FOLD * i + k, TAIL, stride=CH), :] = tail[k * TAIL : (k + 1) * TAIL]
    result[...] = jnp.zeros_like(result)
    lane = lax.broadcasted_iota(jnp.int32, (CH, LANES), 1)

    def take(d, carry):
        begin, length = start_ref[d], length_ref[d]
        row = pl.multiple_of(lax.shift_right_logical(begin, 7) * CH, CH)
        turn = begin & (LANES - 1)
        back = (LANES - turn) & (LANES - 1)
        pieces = [pltpu.roll(seq[pl.ds(row + CH * i, CH), :], back, 1) for i in range(3)]
        whole = lane < LANES - turn
        near = jnp.where(whole, pieces[0], pieces[1])
        far = jnp.where(whole, pieces[1], pieces[2])
        first[pl.ds(d, CH, stride=PEERS), :] = jnp.where(lane < length, near, 0.0)
        second[pl.ds(d, CH, stride=PEERS), :] = jnp.where(lane < length - LANES, far, 0.0)
        return carry

    lax.fori_loop(0, PEERS, take, 0, unroll=8)
    for c in range(CH):
        rows = slice(c * PEERS, (c + 1) * PEERS)
        near, far = first[rows, :], second[rows, :]
        both = jnp.concatenate([near, far], axis=1).astype(BF16)
        done = jnp.dot(both, toep_ref[c], preferred_element_type=F32)
        gain = skip_ref[c]
        first[rows, :] = (done[:, :LANES] + gain * near).astype(BF16).astype(F32)
        second[rows, :] = (done[:, LANES:] + gain * far).astype(BF16).astype(F32)

    def give(d, carry):
        begin, length = start_ref[d], length_ref[d]
        row = pl.multiple_of(lax.shift_right_logical(begin, 7) * CH, CH)
        turn = begin & (LANES - 1)
        near = jnp.where(lane < length, first[pl.ds(d, CH, stride=PEERS), :], 0.0)
        far = jnp.where(lane < length - LANES, second[pl.ds(d, CH, stride=PEERS), :], 0.0)
        near = pltpu.roll(near, turn, 1)
        far = pltpu.roll(far, turn, 1)
        whole = lane >= turn
        result[pl.ds(row, CH), :] += jnp.where(whole, near, 0.0)
        result[pl.ds(row + CH, CH), :] += jnp.where(whole, far, near)
        result[pl.ds(row + 2 * CH, CH), :] += jnp.where(whole, 0.0, far)
        return carry

    lax.fori_loop(0, PEERS, give, 0, unroll=8)
    for c in range(CH):
        msg[pl.ds(c, PEERS, stride=PER), :] = result[pl.ds(c, HEAD, stride=CH), :].T
    for i in range(CH // FOLD):
        parts = [result[pl.ds(HEAD * CH + FOLD * i + k, TAIL, stride=CH), :] for k in range(FOLD)]
        msg[pl.ds(CH + i, PEERS, stride=PER), :] = jnp.concatenate(parts, axis=0).T
    out_ref[...] = msg[...].astype(BF16)


def gate_kernel(in_ref, g_ref, out_ref, msg, low):
    msg[...] = in_ref[...].astype(F32)
    for i in range(CH // FOLD):
        tail = msg[pl.ds(CH + i, PEERS, stride=PER), :]
        for k in range(FOLD):
            low[pl.ds(FOLD * i + k, PEERS, stride=CH), :TAIL] = tail[:, k * TAIL : (k + 1) * TAIL]
    for j in range(8):
        cols = slice(j * LANES, (j + 1) * LANES)
        head = [msg[pl.ds((16 * j + g) * PER, CH), :] for g in range(16)]
        head = jnp.concatenate(head, axis=0).T
        head = (head * g_ref[:HEAD, cols].astype(F32)).astype(BF16)
        tail = low[cols, :].T[:TAIL]
        tail = (tail * g_ref[HEAD:, cols].astype(F32)).astype(BF16)
        for q in range(out_ref.shape[0]):
            out_ref[q, :HEAD, cols] = head
            out_ref[q, HEAD:, cols] = tail


def product_kernel(near, rows_ref, w_ref, out_ref):
    groups, _, width = rows_ref.shape
    total = jnp.zeros((w_ref.shape[0], ROWS), F32)
    for q in range(groups):
        part = w_ref[:, q * width : (q + 1) * width]
        total += lax.dot_general(part, rows_ref[q], (((1,), (1,)), ((), ())), preferred_element_type=F32)
    for j in range(w_ref.shape[0] // LANES):
        parts = []
        for y in range(8):
            for core in range(2):
                group = 16 * j + y // near * 2 * near + core * near + y % near
                parts.append(total[group * CH : (group + 1) * CH])
        block = jnp.concatenate(parts, axis=0)
        out_ref[:, j * LANES : (j + 1) * LANES] = block.T.astype(BF16)


def product(rows, table, near):
    block = 256
    return pl.pallas_call(
        functools.partial(product_kernel, near),
        out_shape=jax.ShapeDtypeStruct((ROWS, table.shape[0]), BF16),
        grid=(table.shape[0] // block,),
        in_specs=[
            pl.BlockSpec(rows.shape, lambda j: (0, 0, 0)),
            pl.BlockSpec((block, table.shape[1]), lambda j: (j, 0)),
        ],
        out_specs=pl.BlockSpec((ROWS, block), lambda j: (0, j)),
        compiler_params=pltpu.CompilerParams(vmem_limit_bytes=VMEM_LIMIT),
        cost_estimate=pl.CostEstimate(
            flops=2 * ROWS * table.size,
            bytes_accessed=2 * (table.size + rows.size + ROWS * table.shape[0]),
            transcendentals=0,
        ),
    )(rows, table)


def exchange(message):
    sent = message.reshape(PEERS, PER // 2, 2, LANES)
    got = lax.all_to_all(sent, SEQ, split_axis=0, concat_axis=0, tiled=True)
    return got.reshape(MSG, LANES)


def local(values, gates, filters, skip, weights, doc_lengths):
    index = lax.axis_index(SEQ).astype(jnp.int32)
    width = values.shape[2]
    msg = jax.ShapeDtypeStruct((MSG, LANES), BF16)
    buf = pltpu.VMEM((MSG, LANES), F32)
    low = pltpu.VMEM((width, LANES), F32)
    packed = call(pack_kernel, msg, [values.reshape(ROWS, width)], [buf, low])
    table = gather_columns(weights.T)
    packed, filters, doc_lengths, skip = lax.optimization_barrier((packed, filters, doc_lengths, skip))
    toep = call(
        toeplitz_kernel,
        jax.ShapeDtypeStruct((CH, 2 * LANES, 2 * LANES), BF16),
        [index[None], filters],
        [pltpu.VMEM((LANES, 2 * LANES), F32)],
        smem=1,
    )
    starts = jnp.cumsum(doc_lengths) - doc_lengths
    own_skip = lax.dynamic_slice(skip, (index * CH,), (CH,))
    got, toep, starts, own_skip = lax.optimization_barrier((exchange(packed), toep, starts, own_skip))
    convolved = call(
        conv_kernel,
        msg,
        [starts, doc_lengths, own_skip, got, toep],
        [
            buf,
            pltpu.VMEM((MSG + 3 * CH, LANES), F32),
            pltpu.VMEM((MSG + 3 * CH, LANES), F32),
            pltpu.VMEM((CH * PEERS, LANES), F32),
            pltpu.VMEM((CH * PEERS, LANES), F32),
        ],
        flops=2 * CH * PEERS * 256 * 256,
        smem=3,
    )
    back = exchange(convolved)
    groups = lax.axis_size("chan")
    copies = call(
        gate_kernel,
        jax.ShapeDtypeStruct((groups, ROWS, width), BF16),
        [back, gates.reshape(ROWS, width)],
        [buf, low],
    )
    rows = lax.all_to_all(copies, "chan", split_axis=0, concat_axis=0, tiled=True)
    mixed = product(rows, table, NEAR)
    return mixed[:, None, :]


def gather_columns(shard):
    shard = lax.all_gather(shard, "y_near", axis=0, tiled=True)
    return lax.all_gather(shard, ("z", "y_far", "core"), axis=0, tiled=True)


def solution(mesh):
    shape = dict(z=8, y_far=8 // NEAR, y_near=NEAR, core=2, chan=4)
    fine = Mesh(mesh.devices.reshape(tuple(shape.values())), tuple(shape))
    placed = (
        P(None, SEQ, "chan"),
        P(None, SEQ, "chan"),
        P(None, "chan"),
        P("chan"),
        P(None, ("chan",) + SEQ),
        P(),
    )
    return jax.shard_map(
        local, mesh=fine, in_specs=placed, out_specs=P(None, SEQ, "chan"), check_vma=False
    )
```

```python
import functools

import jax
import jax.numpy as jnp
from jax import lax
from jax.experimental import pallas as pl
from jax.experimental.pallas import tpu as pltpu
from jax.sharding import Mesh
from jax.sharding import PartitionSpec as P

F32 = jnp.float32
BF16 = jnp.bfloat16
LANES = 128
CH = 8
ROWS = 160
HEAD = 128
TAIL = ROWS - HEAD
FOLD = LANES // TAIL
PER = CH + CH // FOLD
PEERS = 128
MSG = PEERS * PER
VMEM_LIMIT = 48 * 1024 * 1024
SEQ = ("z", "y_half", "y_rest", "core")


def full(shape):
    return pl.BlockSpec(shape, lambda: (0,) * len(shape))


def call(kernel, out, ins, scratch, flops=0, smem=0):
    args = ins
    in_specs = [pl.BlockSpec(memory_space=pltpu.SMEM)] * smem
    in_specs += [full(a.shape) for a in args[smem:]]
    nbytes = sum(a.size * a.dtype.itemsize for a in args)
    nbytes += out.size * out.dtype.itemsize
    return pl.pallas_call(
        kernel,
        out_shape=out,
        in_specs=in_specs,
        out_specs=full(out.shape),
        scratch_shapes=scratch,
        compiler_params=pltpu.CompilerParams(vmem_limit_bytes=VMEM_LIMIT),
        cost_estimate=pl.CostEstimate(flops=flops, bytes_accessed=nbytes, transcendentals=0),
    )(*args)


def pack_kernel(v_ref, out_ref, msg, low):
    for j in range(8):
        cols = slice(j * LANES, (j + 1) * LANES)
        block = v_ref[:, cols].astype(F32)
        head = block[:HEAD].T
        for g in range(16):
            msg[pl.ds((16 * j + g) * PER, CH), :] = head[g * CH : (g + 1) * CH]
        low[cols, :TAIL] = block[HEAD:].T
    for i in range(CH // FOLD):
        parts = [low[pl.ds(FOLD * i + k, PEERS, stride=CH), :][:, :TAIL] for k in range(FOLD)]
        msg[pl.ds(CH + i, PEERS, stride=PER), :] = jnp.concatenate(parts, axis=1)
    out_ref[...] = msg[...].astype(BF16)


def toeplitz_kernel(index_ref, f_ref, out_ref, taps):
    group = index_ref[0]
    tile = pl.multiple_of(lax.div(group, 16) * LANES, LANES)
    taps[...] = f_ref[:, pl.ds(tile, LANES)].astype(F32).T
    mine = taps[pl.ds(pl.multiple_of(lax.rem(group, 16) * CH, CH), CH), :]
    row = lax.broadcasted_iota(jnp.int32, (LANES, LANES), 0)
    lane = lax.broadcasted_iota(jnp.int32, (LANES, LANES), 1)
    for c in range(CH):
        spread = jnp.broadcast_to(mine[c : c + 1, :], (LANES, 2 * LANES))
        turned = pltpu.roll(spread, 0, 1, stride=1, stride_axis=0)
        near = jnp.where(lane >= row, turned[:, :LANES], 0.0).astype(BF16)
        out_ref[c, :LANES, :LANES] = near
        out_ref[c, LANES:, LANES:] = near
        out_ref[c, :LANES, LANES:] = turned[:, LANES:].astype(BF16)
        out_ref[c, LANES:, :LANES] = jnp.zeros((LANES, LANES), BF16)


def conv_kernel(start_ref, length_ref, skip_ref, in_ref, toep_ref, out_ref, msg, seq, result, first, second):
    msg[...] = in_ref[...].astype(F32)
    for c in range(CH):
        seq[pl.ds(c, HEAD, stride=CH), :] = msg[pl.ds(c, PEERS, stride=PER), :].T
    for i in range(CH // FOLD):
        tail = msg[pl.ds(CH + i, PEERS, stride=PER), :].T
        for k in range(FOLD):
            seq[pl.ds(HEAD * CH + FOLD * i + k, TAIL, stride=CH), :] = tail[k * TAIL : (k + 1) * TAIL]
    result[...] = jnp.zeros_like(result)
    lane = lax.broadcasted_iota(jnp.int32, (CH, LANES), 1)

    def take(d, carry):
        begin, length = start_ref[d], length_ref[d]
        row = pl.multiple_of(lax.shift_right_logical(begin, 7) * CH, CH)
        turn = begin & (LANES - 1)
        back = (LANES - turn) & (LANES - 1)
        pieces = [pltpu.roll(seq[pl.ds(row + CH * i, CH), :], back, 1) for i in range(3)]
        whole = lane < LANES - turn
        near = jnp.where(whole, pieces[0], pieces[1])
        far = jnp.where(whole, pieces[1], pieces[2])
        first[pl.ds(d, CH, stride=PEERS), :] = jnp.where(lane < length, near, 0.0)
        second[pl.ds(d, CH, stride=PEERS), :] = jnp.where(lane < length - LANES, far, 0.0)
        return carry

    lax.fori_loop(0, PEERS, take, 0, unroll=8)
    for c in range(CH):
        rows = slice(c * PEERS, (c + 1) * PEERS)
        near, far = first[rows, :], second[rows, :]
        both = jnp.concatenate([near, far], axis=1).astype(BF16)
        done = jnp.dot(both, toep_ref[c], preferred_element_type=F32)
        gain = skip_ref[c]
        first[rows, :] = (done[:, :LANES] + gain * near).astype(BF16).astype(F32)
        second[rows, :] = (done[:, LANES:] + gain * far).astype(BF16).astype(F32)

    def give(d, carry):
        begin, length = start_ref[d], length_ref[d]
        row = pl.multiple_of(lax.shift_right_logical(begin, 7) * CH, CH)
        turn = begin & (LANES - 1)
        near = jnp.where(lane < length, first[pl.ds(d, CH, stride=PEERS), :], 0.0)
        far = jnp.where(lane < length - LANES, second[pl.ds(d, CH, stride=PEERS), :], 0.0)
        near = pltpu.roll(near, turn, 1)
        far = pltpu.roll(far, turn, 1)
        whole = lane >= turn
        result[pl.ds(row, CH), :] += jnp.where(whole, near, 0.0)
        result[pl.ds(row + CH, CH), :] += jnp.where(whole, far, near)
        result[pl.ds(row + 2 * CH, CH), :] += jnp.where(whole, 0.0, far)
        return carry

    lax.fori_loop(0, PEERS, give, 0, unroll=8)
    for c in range(CH):
        msg[pl.ds(c, PEERS, stride=PER), :] = result[pl.ds(c, HEAD, stride=CH), :].T
    for i in range(CH // FOLD):
        parts = [result[pl.ds(HEAD * CH + FOLD * i + k, TAIL, stride=CH), :] for k in range(FOLD)]
        msg[pl.ds(CH + i, PEERS, stride=PER), :] = jnp.concatenate(parts, axis=0).T
    out_ref[...] = msg[...].astype(BF16)


def gate_kernel(in_ref, g_ref, out_ref, msg, low):
    msg[...] = in_ref[...].astype(F32)
    for i in range(CH // FOLD):
        tail = msg[pl.ds(CH + i, PEERS, stride=PER), :]
        for k in range(FOLD):
            low[pl.ds(FOLD * i + k, PEERS, stride=CH), :TAIL] = tail[:, k * TAIL : (k + 1) * TAIL]
    for j in range(8):
        cols = slice(j * LANES, (j + 1) * LANES)
        head = [msg[pl.ds((16 * j + g) * PER, CH), :] for g in range(16)]
        head = jnp.concatenate(head, axis=0).T
        head = (head * g_ref[:HEAD, cols].astype(F32)).astype(BF16)
        tail = low[cols, :].T[:TAIL]
        tail = (tail * g_ref[HEAD:, cols].astype(F32)).astype(BF16)
        for q in range(out_ref.shape[0]):
            out_ref[q, :HEAD, cols] = head
            out_ref[q, HEAD:, cols] = tail


def product_kernel(rows_ref, *refs):
    *w_refs, out_ref = refs
    total = jnp.zeros((w_refs[0].shape[0], ROWS), F32)
    for q, w_ref in enumerate(w_refs):
        total += lax.dot_general(w_ref[...], rows_ref[q], (((1,), (1,)), ((), ())), preferred_element_type=F32)
    for j in range(w_refs[0].shape[0] // LANES):
        parts = []
        for y in range(8):
            for core in range(2):
                group = 16 * j + 4 * (y % 4) + 2 * core + y // 4
                parts.append(total[group * CH : (group + 1) * CH])
        block = jnp.concatenate(parts, axis=0)
        out_ref[:, j * LANES : (j + 1) * LANES] = block.T.astype(BF16)


def product(rows, table):
    block = 256
    groups, _, width = rows.shape
    streams = [pl.BlockSpec((block, width), functools.partial(lambda q, j: (j, q), q)) for q in range(groups)]
    return pl.pallas_call(
        product_kernel,
        out_shape=jax.ShapeDtypeStruct((ROWS, table.shape[0]), BF16),
        grid=(table.shape[0] // block,),
        in_specs=[pl.BlockSpec(rows.shape, lambda j: (0, 0, 0)), *streams],
        out_specs=pl.BlockSpec((ROWS, block), lambda j: (0, j)),
        compiler_params=pltpu.CompilerParams(vmem_limit_bytes=VMEM_LIMIT),
        cost_estimate=pl.CostEstimate(
            flops=2 * ROWS * table.size,
            bytes_accessed=2 * (table.size + rows.size + ROWS * table.shape[0]),
            transcendentals=0,
        ),
    )(rows, *[table] * groups)


def exchange(message):
    sent = message.reshape(PEERS, PER // 2, 2, LANES)
    got = lax.all_to_all(sent, SEQ, split_axis=0, concat_axis=0, tiled=True)
    return got.reshape(MSG, LANES)


def local(values, gates, filters, skip, weights, doc_lengths):
    index = lax.axis_index(SEQ).astype(jnp.int32)
    width = values.shape[2]
    msg = jax.ShapeDtypeStruct((MSG, LANES), BF16)
    buf = pltpu.VMEM((MSG, LANES), F32)
    low = pltpu.VMEM((width, LANES), F32)
    packed = call(pack_kernel, msg, [values.reshape(ROWS, width)], [buf, low])
    table = gather_columns(weights.T)
    packed, filters, doc_lengths, skip = lax.optimization_barrier((packed, filters, doc_lengths, skip))
    toep = call(
        toeplitz_kernel,
        jax.ShapeDtypeStruct((CH, 2 * LANES, 2 * LANES), BF16),
        [index[None], filters],
        [pltpu.VMEM((LANES, 2 * LANES), F32)],
        smem=1,
    )
    starts = jnp.cumsum(doc_lengths) - doc_lengths
    own_skip = lax.dynamic_slice(skip, (index * CH,), (CH,))
    got, toep, starts, own_skip = lax.optimization_barrier((exchange(packed), toep, starts, own_skip))
    convolved = call(
        conv_kernel,
        msg,
        [starts, doc_lengths, own_skip, got, toep],
        [
            buf,
            pltpu.VMEM((MSG + 3 * CH, LANES), F32),
            pltpu.VMEM((MSG + 3 * CH, LANES), F32),
            pltpu.VMEM((CH * PEERS, LANES), F32),
            pltpu.VMEM((CH * PEERS, LANES), F32),
        ],
        flops=2 * CH * PEERS * 256 * 256,
        smem=3,
    )
    back = exchange(convolved)
    groups = lax.axis_size("chan")
    copies = call(
        gate_kernel,
        jax.ShapeDtypeStruct((groups, ROWS, width), BF16),
        [back, gates.reshape(ROWS, width)],
        [buf, low],
    )
    rows = lax.all_to_all(copies, "chan", split_axis=0, concat_axis=0, tiled=True)
    mixed = product(rows, table)
    return mixed[:, None, :]


def gather_columns(shard):
    pair = lax.all_gather(shard, "y_half", axis=0, tiled=True)
    return lax.all_gather(pair, ("z", "y_rest", "core"), axis=0, tiled=True)


def solution(mesh):
    shape = dict(z=8, y_half=2, y_rest=4, core=2, chan=4)
    fine = Mesh(mesh.devices.reshape(tuple(shape.values())), tuple(shape))
    placed = (
        P(None, SEQ, "chan"),
        P(None, SEQ, "chan"),
        P(None, "chan"),
        P("chan"),
        P(None, ("chan",) + SEQ),
        P(),
    )
    return jax.shard_map(
        local, mesh=fine, in_specs=placed, out_specs=P(None, SEQ, "chan"), check_vma=False
    )
```

```python
import jax
import jax.numpy as jnp
from jax import lax
from jax.experimental import pallas as pl
from jax.experimental.pallas import tpu as pltpu
from jax.sharding import Mesh
from jax.sharding import PartitionSpec as P

F32 = jnp.float32
BF16 = jnp.bfloat16
LANES = 128
CH = 8
ROWS = 160
HEAD = 128
TAIL = ROWS - HEAD
FOLD = LANES // TAIL
PER = CH + CH // FOLD
PEERS = 128
MSG = PEERS * PER
VMEM_LIMIT = 48 * 1024 * 1024
SEQ = ("z", "y", "core")


def full(shape):
    return pl.BlockSpec(shape, lambda: (0,) * len(shape))


def call(kernel, out, ins, scratch, flops=0, smem=0):
    args = ins
    in_specs = [pl.BlockSpec(memory_space=pltpu.SMEM)] * smem
    in_specs += [full(a.shape) for a in args[smem:]]
    nbytes = sum(a.size * a.dtype.itemsize for a in args)
    nbytes += out.size * out.dtype.itemsize
    return pl.pallas_call(
        kernel,
        out_shape=out,
        in_specs=in_specs,
        out_specs=full(out.shape),
        scratch_shapes=scratch,
        compiler_params=pltpu.CompilerParams(vmem_limit_bytes=VMEM_LIMIT),
        cost_estimate=pl.CostEstimate(flops=flops, bytes_accessed=nbytes, transcendentals=0),
    )(*args)


def pack_kernel(v_ref, out_ref, msg, low):
    for j in range(8):
        cols = slice(j * LANES, (j + 1) * LANES)
        block = v_ref[:, cols].astype(F32)
        head = block[:HEAD].T
        for g in range(16):
            msg[pl.ds((16 * j + g) * PER, CH), :] = head[g * CH : (g + 1) * CH]
        low[cols, :TAIL] = block[HEAD:].T
    for i in range(CH // FOLD):
        parts = [low[pl.ds(FOLD * i + k, PEERS, stride=CH), :][:, :TAIL] for k in range(FOLD)]
        msg[pl.ds(CH + i, PEERS, stride=PER), :] = jnp.concatenate(parts, axis=1)
    out_ref[...] = msg[...].astype(BF16)


def toeplitz_kernel(index_ref, f_ref, out_ref, taps):
    group = index_ref[0]
    tile = pl.multiple_of(lax.div(group, 16) * LANES, LANES)
    taps[...] = f_ref[:, pl.ds(tile, LANES)].astype(F32).T
    mine = taps[pl.ds(pl.multiple_of(lax.rem(group, 16) * CH, CH), CH), :]
    row = lax.broadcasted_iota(jnp.int32, (LANES, LANES), 0)
    lane = lax.broadcasted_iota(jnp.int32, (LANES, LANES), 1)
    for c in range(CH):
        spread = jnp.broadcast_to(mine[c : c + 1, :], (LANES, 2 * LANES))
        turned = pltpu.roll(spread, 0, 1, stride=1, stride_axis=0)
        near = jnp.where(lane >= row, turned[:, :LANES], 0.0).astype(BF16)
        out_ref[c, :LANES, :LANES] = near
        out_ref[c, LANES:, LANES:] = near
        out_ref[c, :LANES, LANES:] = turned[:, LANES:].astype(BF16)
        out_ref[c, LANES:, :LANES] = jnp.zeros((LANES, LANES), BF16)


def conv_kernel(start_ref, length_ref, skip_ref, in_ref, toep_ref, out_ref, msg, seq, result, first, second):
    msg[...] = in_ref[...].astype(F32)
    for c in range(CH):
        seq[pl.ds(c, HEAD, stride=CH), :] = msg[pl.ds(c, PEERS, stride=PER), :].T
    for i in range(CH // FOLD):
        tail = msg[pl.ds(CH + i, PEERS, stride=PER), :].T
        for k in range(FOLD):
            seq[pl.ds(HEAD * CH + FOLD * i + k, TAIL, stride=CH), :] = tail[k * TAIL : (k + 1) * TAIL]
    result[...] = jnp.zeros_like(result)
    lane = lax.broadcasted_iota(jnp.int32, (CH, LANES), 1)

    def take(d, carry):
        begin, length = start_ref[d], length_ref[d]
        row = pl.multiple_of(lax.shift_right_logical(begin, 7) * CH, CH)
        turn = begin & (LANES - 1)
        back = (LANES - turn) & (LANES - 1)
        pieces = [pltpu.roll(seq[pl.ds(row + CH * i, CH), :], back, 1) for i in range(3)]
        whole = lane < LANES - turn
        near = jnp.where(whole, pieces[0], pieces[1])
        far = jnp.where(whole, pieces[1], pieces[2])
        first[pl.ds(d, CH, stride=PEERS), :] = jnp.where(lane < length, near, 0.0)
        second[pl.ds(d, CH, stride=PEERS), :] = jnp.where(lane < length - LANES, far, 0.0)
        return carry

    lax.fori_loop(0, PEERS, take, 0, unroll=8)
    for c in range(CH):
        rows = slice(c * PEERS, (c + 1) * PEERS)
        near, far = first[rows, :], second[rows, :]
        both = jnp.concatenate([near, far], axis=1).astype(BF16)
        done = jnp.dot(both, toep_ref[c], preferred_element_type=F32)
        gain = skip_ref[c]
        first[rows, :] = (done[:, :LANES] + gain * near).astype(BF16).astype(F32)
        second[rows, :] = (done[:, LANES:] + gain * far).astype(BF16).astype(F32)

    def give(d, carry):
        begin, length = start_ref[d], length_ref[d]
        row = pl.multiple_of(lax.shift_right_logical(begin, 7) * CH, CH)
        turn = begin & (LANES - 1)
        near = jnp.where(lane < length, first[pl.ds(d, CH, stride=PEERS), :], 0.0)
        far = jnp.where(lane < length - LANES, second[pl.ds(d, CH, stride=PEERS), :], 0.0)
        near = pltpu.roll(near, turn, 1)
        far = pltpu.roll(far, turn, 1)
        whole = lane >= turn
        result[pl.ds(row, CH), :] += jnp.where(whole, near, 0.0)
        result[pl.ds(row + CH, CH), :] += jnp.where(whole, far, near)
        result[pl.ds(row + 2 * CH, CH), :] += jnp.where(whole, 0.0, far)
        return carry

    lax.fori_loop(0, PEERS, give, 0, unroll=8)
    for c in range(CH):
        msg[pl.ds(c, PEERS, stride=PER), :] = result[pl.ds(c, HEAD, stride=CH), :].T
    for i in range(CH // FOLD):
        parts = [result[pl.ds(HEAD * CH + FOLD * i + k, TAIL, stride=CH), :] for k in range(FOLD)]
        msg[pl.ds(CH + i, PEERS, stride=PER), :] = jnp.concatenate(parts, axis=0).T
    out_ref[...] = msg[...].astype(BF16)


def gate_kernel(in_ref, g_ref, out_ref, msg, low):
    msg[...] = in_ref[...].astype(F32)
    for i in range(CH // FOLD):
        tail = msg[pl.ds(CH + i, PEERS, stride=PER), :]
        for k in range(FOLD):
            low[pl.ds(FOLD * i + k, PEERS, stride=CH), :TAIL] = tail[:, k * TAIL : (k + 1) * TAIL]
    for j in range(8):
        cols = slice(j * LANES, (j + 1) * LANES)
        head = [msg[pl.ds((16 * j + g) * PER, CH), :] for g in range(16)]
        head = jnp.concatenate(head, axis=0).T
        head = (head * g_ref[:HEAD, cols].astype(F32)).astype(BF16)
        tail = low[cols, :].T[:TAIL]
        tail = (tail * g_ref[HEAD:, cols].astype(F32)).astype(BF16)
        for q in range(out_ref.shape[0]):
            out_ref[q, :HEAD, cols] = head
            out_ref[q, HEAD:, cols] = tail


def product_kernel(rows_ref, twin_ref, w_ref, mine_ref, twins_ref, total):
    step = pl.program_id(0)

    def term(ref):
        return lax.dot_general(w_ref[...], ref[0], (((1,), (1,)), ((), ())), preferred_element_type=F32)

    @pl.when(step == 0)
    def _():
        mine_ref[...] = term(rows_ref)
        total[...] = term(twin_ref)

    @pl.when(step > 0)
    def _():
        mine_ref[...] += term(rows_ref)
        total[...] += term(twin_ref)

    @pl.when(step == pl.num_programs(0) - 1)
    def _():
        twins_ref[...] = total[...].astype(BF16)


def product(rows, twin_rows, columns):
    groups, count, width = rows.shape
    wide = columns.shape[0]
    part = pl.BlockSpec((1, count, width), lambda q: (q, 0, 0))
    result = pl.BlockSpec((wide, count), lambda q: (0, 0))
    return pl.pallas_call(
        product_kernel,
        out_shape=[jax.ShapeDtypeStruct((wide, count), F32), jax.ShapeDtypeStruct((wide, count), BF16)],
        grid=(groups,),
        in_specs=[part, part, pl.BlockSpec((wide, width), lambda q: (0, q))],
        out_specs=[result, result],
        scratch_shapes=[pltpu.VMEM((wide, count), F32)],
        compiler_params=pltpu.CompilerParams(vmem_limit_bytes=VMEM_LIMIT),
        cost_estimate=pl.CostEstimate(
            flops=4 * count * columns.size,
            bytes_accessed=2 * (columns.size + 2 * rows.size + 3 * wide * count),
            transcendentals=0,
        ),
    )(rows, twin_rows, columns)


def join_kernel(core_ref, mine_ref, other_ref, out_ref, zero, one):
    other = other_ref[...].astype(F32)
    first = core_ref[0] == 0
    mine = mine_ref[...]
    zero[...] = jnp.where(first, mine, other)
    one[...] = jnp.where(first, other, mine)
    for z in range(8):
        parts = []
        for y in range(8):
            rows = slice((8 * z + y) * CH, (8 * z + y + 1) * CH)
            parts += [zero[rows, :], one[rows, :]]
        block = jnp.concatenate(parts, axis=0)
        out_ref[:, z * LANES : (z + 1) * LANES] = block.T.astype(BF16)


def exchange(message):
    sent = message.reshape(PEERS, PER // 2, 2, LANES)
    got = lax.all_to_all(sent, SEQ, split_axis=0, concat_axis=0, tiled=True)
    return got.reshape(MSG, LANES)


def local(values, gates, filters, skip, weights, doc_lengths):
    index = lax.axis_index(SEQ).astype(jnp.int32)
    width = values.shape[2]
    msg = jax.ShapeDtypeStruct((MSG, LANES), BF16)
    buf = pltpu.VMEM((MSG, LANES), F32)
    low = pltpu.VMEM((width, LANES), F32)
    packed = call(pack_kernel, msg, [values.reshape(ROWS, width)], [buf, low])
    table = gather_columns(weights.T)
    packed, filters, doc_lengths, skip = lax.optimization_barrier((packed, filters, doc_lengths, skip))
    toep = call(
        toeplitz_kernel,
        jax.ShapeDtypeStruct((CH, 2 * LANES, 2 * LANES), BF16),
        [index[None], filters],
        [pltpu.VMEM((LANES, 2 * LANES), F32)],
        smem=1,
    )
    starts = jnp.cumsum(doc_lengths) - doc_lengths
    own_skip = lax.dynamic_slice(skip, (index * CH,), (CH,))
    got, toep, starts, own_skip = lax.optimization_barrier((exchange(packed), toep, starts, own_skip))
    convolved = call(
        conv_kernel,
        msg,
        [starts, doc_lengths, own_skip, got, toep],
        [
            buf,
            pltpu.VMEM((MSG + 3 * CH, LANES), F32),
            pltpu.VMEM((MSG + 3 * CH, LANES), F32),
            pltpu.VMEM((CH * PEERS, LANES), F32),
            pltpu.VMEM((CH * PEERS, LANES), F32),
        ],
        flops=2 * CH * PEERS * 256 * 256,
        smem=3,
    )
    back = exchange(convolved)
    groups = lax.axis_size("chan")
    copies = call(
        gate_kernel,
        jax.ShapeDtypeStruct((groups, ROWS, width), BF16),
        [back, gates.reshape(ROWS, width)],
        [buf, low],
    )
    rows = lax.all_to_all(copies, "chan", split_axis=0, concat_axis=0, tiled=True)
    swap = [(0, 1), (1, 0)]
    mine, twins = product(rows, lax.ppermute(rows, "core", swap), table)
    place = pltpu.VMEM(mine.shape, F32)
    mixed = call(
        join_kernel,
        jax.ShapeDtypeStruct((ROWS, width), BF16),
        [lax.rem(index, 2)[None], mine, lax.ppermute(twins, "core", swap)],
        [place, place],
        smem=1,
    )
    return mixed[:, None, :]


def gather_columns(shard):
    return lax.all_gather(shard, ("z", "y"), axis=0, tiled=True)


def solution(mesh):
    shape = dict(z=8, y=8, core=2, chan=4)
    fine = Mesh(mesh.devices.reshape(tuple(shape.values())), tuple(shape))
    placed = (
        P(None, SEQ, "chan"),
        P(None, SEQ, "chan"),
        P(None, "chan"),
        P("chan"),
        P(None, ("chan",) + SEQ),
        P(),
    )
    return jax.shard_map(
        local, mesh=fine, in_specs=placed, out_specs=P(None, SEQ, "chan"), check_vma=False
    )
```

```python
import functools

import jax
import jax.numpy as jnp
from jax import lax
from jax.experimental import pallas as pl
from jax.experimental.pallas import tpu as pltpu
from jax.sharding import PartitionSpec as P

F32 = jnp.float32
BF16 = jnp.bfloat16
LANES = 128
CH = 8
ROWS = 160
HEAD = 128
TAIL = ROWS - HEAD
FOLD = LANES // TAIL
PER = CH + CH // FOLD
PEERS = 128
MSG = PEERS * PER
VMEM_LIMIT = 48 * 1024 * 1024
SEQ = "seq"
LINE = 8
AWAY = (0, 4, 2, -2, 1, 3, -1, -3)


def full(shape):
    return pl.BlockSpec(shape, lambda: (0,) * len(shape))


def call(kernel, out, ins, scratch, flops=0, smem=0):
    args = ins
    in_specs = [pl.BlockSpec(memory_space=pltpu.SMEM)] * smem
    in_specs += [full(a.shape) for a in args[smem:]]
    nbytes = sum(a.size * a.dtype.itemsize for a in args)
    nbytes += out.size * out.dtype.itemsize
    return pl.pallas_call(
        kernel,
        out_shape=out,
        in_specs=in_specs,
        out_specs=full(out.shape),
        scratch_shapes=scratch,
        compiler_params=pltpu.CompilerParams(vmem_limit_bytes=VMEM_LIMIT),
        cost_estimate=pl.CostEstimate(flops=flops, bytes_accessed=nbytes, transcendentals=0),
    )(*args)


def pack_kernel(v_ref, out_ref, msg, low):
    for j in range(8):
        cols = slice(j * LANES, (j + 1) * LANES)
        block = v_ref[:, cols].astype(F32)
        head = block[:HEAD].T
        for g in range(16):
            msg[pl.ds((16 * j + g) * PER, CH), :] = head[g * CH : (g + 1) * CH]
        low[cols, :TAIL] = block[HEAD:].T
    for i in range(CH // FOLD):
        parts = [low[pl.ds(FOLD * i + k, PEERS, stride=CH), :][:, :TAIL] for k in range(FOLD)]
        msg[pl.ds(CH + i, PEERS, stride=PER), :] = jnp.concatenate(parts, axis=1)
    out_ref[...] = msg[...].astype(BF16)


def toeplitz_kernel(index_ref, f_ref, out_ref, taps):
    group = index_ref[0]
    tile = pl.multiple_of(lax.div(group, 16) * LANES, LANES)
    taps[...] = f_ref[:, pl.ds(tile, LANES)].astype(F32).T
    mine = taps[pl.ds(pl.multiple_of(lax.rem(group, 16) * CH, CH), CH), :]
    row = lax.broadcasted_iota(jnp.int32, (LANES, LANES), 0)
    lane = lax.broadcasted_iota(jnp.int32, (LANES, LANES), 1)
    for c in range(CH):
        spread = jnp.broadcast_to(mine[c : c + 1, :], (LANES, 2 * LANES))
        turned = pltpu.roll(spread, 0, 1, stride=1, stride_axis=0)
        near = jnp.where(lane >= row, turned[:, :LANES], 0.0).astype(BF16)
        out_ref[c, :LANES, :LANES] = near
        out_ref[c, LANES:, LANES:] = near
        out_ref[c, :LANES, LANES:] = turned[:, LANES:].astype(BF16)
        out_ref[c, LANES:, :LANES] = jnp.zeros((LANES, LANES), BF16)


def conv_kernel(start_ref, length_ref, skip_ref, in_ref, toep_ref, out_ref, msg, seq, result, first, second):
    msg[...] = in_ref[...].astype(F32)
    for c in range(CH):
        seq[pl.ds(c, HEAD, stride=CH), :] = msg[pl.ds(c, PEERS, stride=PER), :].T
    for i in range(CH // FOLD):
        tail = msg[pl.ds(CH + i, PEERS, stride=PER), :].T
        for k in range(FOLD):
            seq[pl.ds(HEAD * CH + FOLD * i + k, TAIL, stride=CH), :] = tail[k * TAIL : (k + 1) * TAIL]
    result[...] = jnp.zeros_like(result)
    lane = lax.broadcasted_iota(jnp.int32, (CH, LANES), 1)

    def take(d, carry):
        begin, length = start_ref[d], length_ref[d]
        row = pl.multiple_of(lax.shift_right_logical(begin, 7) * CH, CH)
        turn = begin & (LANES - 1)
        back = (LANES - turn) & (LANES - 1)
        pieces = [pltpu.roll(seq[pl.ds(row + CH * i, CH), :], back, 1) for i in range(3)]
        whole = lane < LANES - turn
        near = jnp.where(whole, pieces[0], pieces[1])
        far = jnp.where(whole, pieces[1], pieces[2])
        first[pl.ds(d, CH, stride=PEERS), :] = jnp.where(lane < length, near, 0.0)
        second[pl.ds(d, CH, stride=PEERS), :] = jnp.where(lane < length - LANES, far, 0.0)
        return carry

    lax.fori_loop(0, PEERS, take, 0, unroll=8)
    for c in range(CH):
        rows = slice(c * PEERS, (c + 1) * PEERS)
        near, far = first[rows, :], second[rows, :]
        both = jnp.concatenate([near, far], axis=1).astype(BF16)
        done = jnp.dot(both, toep_ref[c], preferred_element_type=F32)
        gain = skip_ref[c]
        first[rows, :] = (done[:, :LANES] + gain * near).astype(BF16).astype(F32)
        second[rows, :] = (done[:, LANES:] + gain * far).astype(BF16).astype(F32)

    def give(d, carry):
        begin, length = start_ref[d], length_ref[d]
        row = pl.multiple_of(lax.shift_right_logical(begin, 7) * CH, CH)
        turn = begin & (LANES - 1)
        near = jnp.where(lane < length, first[pl.ds(d, CH, stride=PEERS), :], 0.0)
        far = jnp.where(lane < length - LANES, second[pl.ds(d, CH, stride=PEERS), :], 0.0)
        near = pltpu.roll(near, turn, 1)
        far = pltpu.roll(far, turn, 1)
        whole = lane >= turn
        result[pl.ds(row, CH), :] += jnp.where(whole, near, 0.0)
        result[pl.ds(row + CH, CH), :] += jnp.where(whole, far, near)
        result[pl.ds(row + 2 * CH, CH), :] += jnp.where(whole, 0.0, far)
        return carry

    lax.fori_loop(0, PEERS, give, 0, unroll=8)
    for c in range(CH):
        msg[pl.ds(c, PEERS, stride=PER), :] = result[pl.ds(c, HEAD, stride=CH), :].T
    for i in range(CH // FOLD):
        parts = [result[pl.ds(HEAD * CH + FOLD * i + k, TAIL, stride=CH), :] for k in range(FOLD)]
        msg[pl.ds(CH + i, PEERS, stride=PER), :] = jnp.concatenate(parts, axis=0).T
    out_ref[...] = msg[...].astype(BF16)


def gate_kernel(in_ref, g_ref, out_ref, msg, low):
    msg[...] = in_ref[...].astype(F32)
    for i in range(CH // FOLD):
        tail = msg[pl.ds(CH + i, PEERS, stride=PER), :]
        for k in range(FOLD):
            low[pl.ds(FOLD * i + k, PEERS, stride=CH), :TAIL] = tail[:, k * TAIL : (k + 1) * TAIL]
    for j in range(8):
        cols = slice(j * LANES, (j + 1) * LANES)
        head = [msg[pl.ds((16 * j + g) * PER, CH), :] for g in range(16)]
        head = jnp.concatenate(head, axis=0).T
        head = (head * g_ref[:HEAD, cols].astype(F32)).astype(BF16)
        tail = low[cols, :].T[:TAIL]
        tail = (tail * g_ref[HEAD:, cols].astype(F32)).astype(BF16)
        for q in range(out_ref.shape[0]):
            out_ref[q, :HEAD, cols] = head
            out_ref[q, HEAD:, cols] = tail


def multiply(rows_ref, w_ref):
    groups, _, width = rows_ref.shape
    total = jnp.zeros((w_ref.shape[0], ROWS), F32)
    for q in range(groups):
        part = w_ref[:, q * width : (q + 1) * width]
        total += lax.dot_general(part, rows_ref[q], (((1,), (1,)), ((), ())), preferred_element_type=F32)
    return total


def own_kernel(rows_ref, near_ref, far_ref, out_ref):
    half = near_ref.shape[0]
    out_ref[:half] = multiply(rows_ref, near_ref)
    out_ref[half:] = multiply(rows_ref, far_ref)


def other_kernel(index_ref, rows_ref, near_ref, far_ref, own_ref, out_ref, other, columns):
    half = near_ref.shape[0]
    other[:half] = multiply(rows_ref, near_ref)
    other[half:] = multiply(rows_ref, far_ref)
    index = index_ref[0]
    z, y, core = lax.shift_right_logical(index, 4), lax.shift_right_logical(index, 1) & 7, index & 1
    for source, origin in ((own_ref, core), (other, 1 - core)):
        straight = origin == 0
        outer, outer_step = jnp.where(straight, z, y), jnp.where(straight, 16, 2)
        inner, inner_step = jnp.where(straight, y, z), jnp.where(straight, 2, 16)
        inners = [((inner + AWAY[a]) & 7) * inner_step + origin for a in range(LINE)]
        for b in range(LINE):
            base = ((outer + AWAY[b]) & 7) * outer_step
            for a in range(LINE):
                group = base + inners[a]
                rows = slice((LINE * b + a) * CH, (LINE * b + a + 1) * CH)
                columns[pl.ds(pl.multiple_of(group * CH, CH), CH), :] = source[rows, :]
    for j in range(8):
        cols = slice(j * LANES, (j + 1) * LANES)
        out_ref[:, cols] = columns[cols, :].T.astype(BF16)


def exchange(message):
    sent = message.reshape(PEERS, PER // 2, 2, LANES)
    got = lax.all_to_all(sent, SEQ, split_axis=0, concat_axis=0, tiled=True)
    return got.reshape(MSG, LANES)


def local(values, gates, filters, skip, weights, doc_lengths):
    index = lax.axis_index(SEQ).astype(jnp.int32)
    width = values.shape[2]
    msg = jax.ShapeDtypeStruct((MSG, LANES), BF16)
    buf = pltpu.VMEM((MSG, LANES), F32)
    low = pltpu.VMEM((width, LANES), F32)
    packed = call(pack_kernel, msg, [values.reshape(ROWS, width)], [buf, low])
    packed, filters, doc_lengths, skip, shard = lax.optimization_barrier(
        (packed, filters, doc_lengths, skip, weights.T)
    )
    line = first_line(shard)
    toep = call(
        toeplitz_kernel,
        jax.ShapeDtypeStruct((CH, 2 * LANES, 2 * LANES), BF16),
        [index[None], filters],
        [pltpu.VMEM((LANES, 2 * LANES), F32)],
        smem=1,
    )
    starts = jnp.cumsum(doc_lengths) - doc_lengths
    own_skip = lax.dynamic_slice(skip, (index * CH,), (CH,))
    got = exchange(packed)
    line, toep, starts, own_skip = lax.optimization_barrier((line, toep, starts, own_skip))
    fars = direct(line, "z")
    convolved = call(
        conv_kernel,
        msg,
        [starts, doc_lengths, own_skip, got, toep],
        [
            buf,
            pltpu.VMEM((MSG + 3 * CH, LANES), F32),
            pltpu.VMEM((MSG + 3 * CH, LANES), F32),
            pltpu.VMEM((CH * PEERS, LANES), F32),
            pltpu.VMEM((CH * PEERS, LANES), F32),
        ],
        flops=2 * CH * PEERS * 256 * 256,
        smem=3,
    )
    block, four, two, back_two, _ = lax.optimization_barrier((line, *fars, convolved))
    near = jnp.concatenate([block, four, two, back_two], axis=0)
    back = exchange(convolved)
    sides = handed(block, two, back_two, "z")
    groups = lax.axis_size("chan")
    copies = call(
        gate_kernel,
        jax.ShapeDtypeStruct((groups, ROWS, width), BF16),
        [back, gates.reshape(ROWS, width)],
        [buf, low],
    )
    rows = lax.all_to_all(copies, "chan", split_axis=0, concat_axis=0, tiled=True)
    rows, *sides = lax.optimization_barrier((rows, *sides))
    own = near, jnp.concatenate(sides, axis=0)
    other = tuple(lax.ppermute(part, "seq", [(i, i ^ 1) for i in range(PEERS)]) for part in own)
    wide = own[0].shape[0] + own[1].shape[0]
    half = jax.ShapeDtypeStruct((wide, ROWS), F32)
    flops = 2 * ROWS * wide * own[0].shape[1]
    first = call(own_kernel, half, [rows, *own], [], flops=flops)
    mixed = call(
        other_kernel,
        jax.ShapeDtypeStruct((ROWS, width), BF16),
        [index[None], rows, *other, first],
        [pltpu.VMEM((wide, ROWS), F32), pltpu.VMEM((2 * wide, ROWS), F32)],
        flops=flops,
        smem=1,
    )
    return mixed[:, None, :]


def lines(first):
    along = {"y": [], "z": []}
    for core in range(2):
        axis = first if core == 0 else ("z" if first == "y" else "y")
        for fixed in range(8):
            along[axis].append([(fixed * 16 + i * 2 if axis == "y" else i * 16 + fixed * 2) + core for i in range(8)])
    return along["y"] + along["z"]


def move(array, first, places):
    pairs = [(line[(i + places) % LINE], line[i]) for line in lines(first) for i in range(LINE)]
    return lax.ppermute(array, "seq", pairs)


def direct(block, first):
    return tuple(move(block, first, places) for places in AWAY[1:4])


def handed(block, two, back_two, first):
    one = move(jnp.concatenate([block, two], axis=0), first, 1)
    return one, move(jnp.concatenate([block, back_two], axis=0), first, -1)


def first_line(shard):
    four, two, back_two = direct(shard, "y")
    return jnp.concatenate([shard, four, two, back_two, *handed(shard, two, back_two, "y")], axis=0)


def solution(mesh):
    placed = (
        P(None, "seq", "chan"),
        P(None, "seq", "chan"),
        P(None, "chan"),
        P("chan"),
        P(None, ("chan", "seq")),
        P(),
    )
    return jax.shard_map(
        local, mesh=mesh, in_specs=placed, out_specs=P(None, "seq", "chan"), check_vma=False
    )
```

```python
import jax
import jax.numpy as jnp
from jax import lax
from jax.experimental import pallas as pl
from jax.experimental.pallas import tpu as pltpu
from jax.sharding import Mesh
from jax.sharding import PartitionSpec as P

F32 = jnp.float32
BF16 = jnp.bfloat16
LANES = 128
CH = 8
ROWS = 160
HEAD = 128
TAIL = ROWS - HEAD
FOLD = LANES // TAIL
PER = CH + CH // FOLD
PEERS = 128
MSG = PEERS * PER
VMEM_LIMIT = 48 * 1024 * 1024
SEQ = ("z", "y", "core")


def full(shape):
    return pl.BlockSpec(shape, lambda: (0,) * len(shape))


def call(kernel, out, ins, scratch, flops=0, smem=0):
    args = ins
    in_specs = [pl.BlockSpec(memory_space=pltpu.SMEM)] * smem
    in_specs += [full(a.shape) for a in args[smem:]]
    nbytes = sum(a.size * a.dtype.itemsize for a in args)
    nbytes += out.size * out.dtype.itemsize
    return pl.pallas_call(
        kernel,
        out_shape=out,
        in_specs=in_specs,
        out_specs=full(out.shape),
        scratch_shapes=scratch,
        compiler_params=pltpu.CompilerParams(vmem_limit_bytes=VMEM_LIMIT),
        cost_estimate=pl.CostEstimate(flops=flops, bytes_accessed=nbytes, transcendentals=0),
    )(*args)


def pack_kernel(v_ref, out_ref, msg, low):
    for j in range(8):
        cols = slice(j * LANES, (j + 1) * LANES)
        block = v_ref[:, cols].astype(F32)
        head = block[:HEAD].T
        for g in range(16):
            msg[pl.ds((16 * j + g) * PER, CH), :] = head[g * CH : (g + 1) * CH]
        low[cols, :TAIL] = block[HEAD:].T
    for i in range(CH // FOLD):
        parts = [low[pl.ds(FOLD * i + k, PEERS, stride=CH), :][:, :TAIL] for k in range(FOLD)]
        msg[pl.ds(CH + i, PEERS, stride=PER), :] = jnp.concatenate(parts, axis=1)
    out_ref[...] = msg[...].astype(BF16)


def toeplitz_kernel(index_ref, f_ref, out_ref, taps):
    group = index_ref[0]
    tile = pl.multiple_of(lax.div(group, 16) * LANES, LANES)
    taps[...] = f_ref[:, pl.ds(tile, LANES)].astype(F32).T
    mine = taps[pl.ds(pl.multiple_of(lax.rem(group, 16) * CH, CH), CH), :]
    row = lax.broadcasted_iota(jnp.int32, (LANES, LANES), 0)
    lane = lax.broadcasted_iota(jnp.int32, (LANES, LANES), 1)
    for c in range(CH):
        spread = jnp.broadcast_to(mine[c : c + 1, :], (LANES, 2 * LANES))
        turned = pltpu.roll(spread, 0, 1, stride=1, stride_axis=0)
        near = jnp.where(lane >= row, turned[:, :LANES], 0.0).astype(BF16)
        out_ref[c, :LANES, :LANES] = near
        out_ref[c, LANES:, LANES:] = near
        out_ref[c, :LANES, LANES:] = turned[:, LANES:].astype(BF16)
        out_ref[c, LANES:, :LANES] = jnp.zeros((LANES, LANES), BF16)


def conv_kernel(start_ref, length_ref, skip_ref, in_ref, toep_ref, out_ref, msg, seq, result, first, second):
    msg[...] = in_ref[...].astype(F32)
    for c in range(CH):
        seq[pl.ds(c, HEAD, stride=CH), :] = msg[pl.ds(c, PEERS, stride=PER), :].T
    for i in range(CH // FOLD):
        tail = msg[pl.ds(CH + i, PEERS, stride=PER), :].T
        for k in range(FOLD):
            seq[pl.ds(HEAD * CH + FOLD * i + k, TAIL, stride=CH), :] = tail[k * TAIL : (k + 1) * TAIL]
    result[...] = jnp.zeros_like(result)
    lane = lax.broadcasted_iota(jnp.int32, (CH, LANES), 1)

    def take(d, carry):
        begin, length = start_ref[d], length_ref[d]
        row = pl.multiple_of(lax.shift_right_logical(begin, 7) * CH, CH)
        turn = begin & (LANES - 1)
        back = (LANES - turn) & (LANES - 1)
        pieces = [pltpu.roll(seq[pl.ds(row + CH * i, CH), :], back, 1) for i in range(3)]
        whole = lane < LANES - turn
        near = jnp.where(whole, pieces[0], pieces[1])
        far = jnp.where(whole, pieces[1], pieces[2])
        first[pl.ds(d, CH, stride=PEERS), :] = jnp.where(lane < length, near, 0.0)
        second[pl.ds(d, CH, stride=PEERS), :] = jnp.where(lane < length - LANES, far, 0.0)
        return carry

    lax.fori_loop(0, PEERS, take, 0, unroll=8)
    for c in range(CH):
        rows = slice(c * PEERS, (c + 1) * PEERS)
        near, far = first[rows, :], second[rows, :]
        both = jnp.concatenate([near, far], axis=1).astype(BF16)
        done = jnp.dot(both, toep_ref[c], preferred_element_type=F32)
        gain = skip_ref[c]
        first[rows, :] = (done[:, :LANES] + gain * near).astype(BF16).astype(F32)
        second[rows, :] = (done[:, LANES:] + gain * far).astype(BF16).astype(F32)

    def give(d, carry):
        begin, length = start_ref[d], length_ref[d]
        row = pl.multiple_of(lax.shift_right_logical(begin, 7) * CH, CH)
        turn = begin & (LANES - 1)
        near = jnp.where(lane < length, first[pl.ds(d, CH, stride=PEERS), :], 0.0)
        far = jnp.where(lane < length - LANES, second[pl.ds(d, CH, stride=PEERS), :], 0.0)
        near = pltpu.roll(near, turn, 1)
        far = pltpu.roll(far, turn, 1)
        whole = lane >= turn
        result[pl.ds(row, CH), :] += jnp.where(whole, near, 0.0)
        result[pl.ds(row + CH, CH), :] += jnp.where(whole, far, near)
        result[pl.ds(row + 2 * CH, CH), :] += jnp.where(whole, 0.0, far)
        return carry

    lax.fori_loop(0, PEERS, give, 0, unroll=8)
    for c in range(CH):
        msg[pl.ds(c, PEERS, stride=PER), :] = result[pl.ds(c, HEAD, stride=CH), :].T
    for i in range(CH // FOLD):
        parts = [result[pl.ds(HEAD * CH + FOLD * i + k, TAIL, stride=CH), :] for k in range(FOLD)]
        msg[pl.ds(CH + i, PEERS, stride=PER), :] = jnp.concatenate(parts, axis=0).T
    out_ref[...] = msg[...].astype(BF16)


def gate_kernel(in_ref, g_ref, out_ref, msg, low):
    msg[...] = in_ref[...].astype(F32)
    for i in range(CH // FOLD):
        tail = msg[pl.ds(CH + i, PEERS, stride=PER), :]
        for k in range(FOLD):
            low[pl.ds(FOLD * i + k, PEERS, stride=CH), :TAIL] = tail[:, k * TAIL : (k + 1) * TAIL]
    for j in range(8):
        cols = slice(j * LANES, (j + 1) * LANES)
        head = [msg[pl.ds((16 * j + g) * PER, CH), :] for g in range(16)]
        head = jnp.concatenate(head, axis=0).T
        head = (head * g_ref[:HEAD, cols].astype(F32)).astype(BF16)
        tail = low[cols, :].T[:TAIL]
        tail = (tail * g_ref[HEAD:, cols].astype(F32)).astype(BF16)
        for q in range(out_ref.shape[0]):
            out_ref[q, :HEAD, cols] = head
            out_ref[q, HEAD:, cols] = tail


def product_kernel(rows_ref, w_ref, out_ref, total):
    step = pl.program_id(0)
    term = lax.dot_general(w_ref[...], rows_ref[0], (((1,), (1,)), ((), ())), preferred_element_type=F32)

    @pl.when(step == 0)
    def _():
        total[...] = term

    @pl.when(step > 0)
    def _():
        total[...] += term

    @pl.when(step == pl.num_programs(0) - 1)
    def _():
        for j in range(total.shape[0] // LANES):
            cols = slice(j * LANES, (j + 1) * LANES)
            out_ref[:, cols] = total[cols, :].T.astype(BF16)


def product(rows, table):
    block = 512
    count, wide = rows.shape[1], table.shape[0]
    parts = rows.shape[2] // block
    return pl.pallas_call(
        product_kernel,
        out_shape=jax.ShapeDtypeStruct((count, wide), BF16),
        grid=(table.shape[1] // block,),
        in_specs=[
            pl.BlockSpec((1, count, block), lambda k: (k // parts, 0, k % parts)),
            pl.BlockSpec((wide, block), lambda k: (0, k)),
        ],
        out_specs=pl.BlockSpec((count, wide), lambda k: (0, 0)),
        scratch_shapes=[pltpu.VMEM((wide, count), F32)],
        compiler_params=pltpu.CompilerParams(vmem_limit_bytes=VMEM_LIMIT),
        cost_estimate=pl.CostEstimate(
            flops=2 * count * table.size,
            bytes_accessed=2 * (table.size + rows.size + count * wide),
            transcendentals=0,
        ),
    )(rows, table)


def exchange(message):
    sent = message.reshape(PEERS, PER // 2, 2, LANES)
    got = lax.all_to_all(sent, SEQ, split_axis=0, concat_axis=0, tiled=True)
    return got.reshape(MSG, LANES)


def local(values, gates, filters, skip, weights, doc_lengths):
    index = lax.axis_index(SEQ).astype(jnp.int32)
    width = values.shape[2]
    msg = jax.ShapeDtypeStruct((MSG, LANES), BF16)
    buf = pltpu.VMEM((MSG, LANES), F32)
    low = pltpu.VMEM((width, LANES), F32)
    packed = call(pack_kernel, msg, [values.reshape(ROWS, width)], [buf, low])
    table = gather_columns(weights.T)
    packed, filters, doc_lengths, skip = lax.optimization_barrier((packed, filters, doc_lengths, skip))
    toep = call(
        toeplitz_kernel,
        jax.ShapeDtypeStruct((CH, 2 * LANES, 2 * LANES), BF16),
        [index[None], filters],
        [pltpu.VMEM((LANES, 2 * LANES), F32)],
        smem=1,
    )
    starts = jnp.cumsum(doc_lengths) - doc_lengths
    own_skip = lax.dynamic_slice(skip, (index * CH,), (CH,))
    got, toep, starts, own_skip = lax.optimization_barrier((exchange(packed), toep, starts, own_skip))
    convolved = call(
        conv_kernel,
        msg,
        [starts, doc_lengths, own_skip, got, toep],
        [
            buf,
            pltpu.VMEM((MSG + 3 * CH, LANES), F32),
            pltpu.VMEM((MSG + 3 * CH, LANES), F32),
            pltpu.VMEM((CH * PEERS, LANES), F32),
            pltpu.VMEM((CH * PEERS, LANES), F32),
        ],
        flops=2 * CH * PEERS * 256 * 256,
        smem=3,
    )
    back = exchange(convolved)
    groups = lax.axis_size("chan")
    copies = call(
        gate_kernel,
        jax.ShapeDtypeStruct((groups, ROWS, width), BF16),
        [back, gates.reshape(ROWS, width)],
        [buf, low],
    )
    rows = lax.all_to_all(copies, "chan", split_axis=0, concat_axis=0, tiled=True)
    mixed = product(rows, table)
    return mixed[:, None, :]


def gather_columns(shard):
    return lax.all_gather(shard, SEQ, axis=0, tiled=True)


def solution(mesh):
    shape = dict(z=8, y=8, core=2, chan=4)
    fine = Mesh(mesh.devices.reshape(tuple(shape.values())), tuple(shape))
    placed = (
        P(None, SEQ, "chan"),
        P(None, SEQ, "chan"),
        P(None, "chan"),
        P("chan"),
        P(None, ("chan",) + SEQ),
        P(),
    )
    return jax.shard_map(
        local, mesh=fine, in_specs=placed, out_specs=P(None, SEQ, "chan"), check_vma=False
    )
```

```python
import jax
import jax.numpy as jnp
from jax import lax
from jax.experimental import pallas as pl
from jax.experimental.pallas import tpu as pltpu
from jax.sharding import Mesh
from jax.sharding import PartitionSpec as P

F32 = jnp.float32
BF16 = jnp.bfloat16
LANES = 128
CH = 8
ROWS = 160
HEAD = 128
TAIL = ROWS - HEAD
FOLD = LANES // TAIL
PER = CH + CH // FOLD
PEERS = 128
MSG = PEERS * PER
VMEM_LIMIT = 48 * 1024 * 1024
SEQ = ("z", "y", "core")


def full(shape):
    return pl.BlockSpec(shape, lambda: (0,) * len(shape))


def call(kernel, out, ins, scratch, flops=0, smem=0):
    args = ins
    in_specs = [pl.BlockSpec(memory_space=pltpu.SMEM)] * smem
    in_specs += [full(a.shape) for a in args[smem:]]
    nbytes = sum(a.size * a.dtype.itemsize for a in args)
    nbytes += out.size * out.dtype.itemsize
    return pl.pallas_call(
        kernel,
        out_shape=out,
        in_specs=in_specs,
        out_specs=full(out.shape),
        scratch_shapes=scratch,
        compiler_params=pltpu.CompilerParams(vmem_limit_bytes=VMEM_LIMIT),
        cost_estimate=pl.CostEstimate(flops=flops, bytes_accessed=nbytes, transcendentals=0),
    )(*args)


def pack_kernel(v_ref, out_ref, msg, low):
    for j in range(8):
        cols = slice(j * LANES, (j + 1) * LANES)
        block = v_ref[:, cols].astype(F32)
        head = block[:HEAD].T
        for g in range(16):
            msg[pl.ds((16 * j + g) * PER, CH), :] = head[g * CH : (g + 1) * CH]
        low[cols, :TAIL] = block[HEAD:].T
    for i in range(CH // FOLD):
        parts = [low[pl.ds(FOLD * i + k, PEERS, stride=CH), :][:, :TAIL] for k in range(FOLD)]
        msg[pl.ds(CH + i, PEERS, stride=PER), :] = jnp.concatenate(parts, axis=1)
    out_ref[...] = msg[...].astype(BF16)


def toeplitz_kernel(index_ref, f_ref, out_ref, taps):
    group = index_ref[0]
    tile = pl.multiple_of(lax.div(group, 16) * LANES, LANES)
    taps[...] = f_ref[:, pl.ds(tile, LANES)].astype(F32).T
    mine = taps[pl.ds(pl.multiple_of(lax.rem(group, 16) * CH, CH), CH), :]
    row = lax.broadcasted_iota(jnp.int32, (LANES, LANES), 0)
    lane = lax.broadcasted_iota(jnp.int32, (LANES, LANES), 1)
    for c in range(CH):
        spread = jnp.broadcast_to(mine[c : c + 1, :], (LANES, 2 * LANES))
        turned = pltpu.roll(spread, 0, 1, stride=1, stride_axis=0)
        near = jnp.where(lane >= row, turned[:, :LANES], 0.0).astype(BF16)
        out_ref[c, :LANES, :LANES] = near
        out_ref[c, LANES:, LANES:] = near
        out_ref[c, :LANES, LANES:] = turned[:, LANES:].astype(BF16)
        out_ref[c, LANES:, :LANES] = jnp.zeros((LANES, LANES), BF16)


def conv_kernel(start_ref, length_ref, skip_ref, in_ref, toep_ref, out_ref, msg, seq, result, first, second):
    msg[...] = in_ref[...].astype(F32)
    for c in range(CH):
        seq[pl.ds(c, HEAD, stride=CH), :] = msg[pl.ds(c, PEERS, stride=PER), :].T
    for i in range(CH // FOLD):
        tail = msg[pl.ds(CH + i, PEERS, stride=PER), :].T
        for k in range(FOLD):
            seq[pl.ds(HEAD * CH + FOLD * i + k, TAIL, stride=CH), :] = tail[k * TAIL : (k + 1) * TAIL]
    result[...] = jnp.zeros_like(result)
    lane = lax.broadcasted_iota(jnp.int32, (CH, LANES), 1)

    def take(d, carry):
        begin, length = start_ref[d], length_ref[d]
        row = pl.multiple_of(lax.shift_right_logical(begin, 7) * CH, CH)
        turn = begin & (LANES - 1)
        back = (LANES - turn) & (LANES - 1)
        pieces = [pltpu.roll(seq[pl.ds(row + CH * i, CH), :], back, 1) for i in range(3)]
        whole = lane < LANES - turn
        near = jnp.where(whole, pieces[0], pieces[1])
        far = jnp.where(whole, pieces[1], pieces[2])
        first[pl.ds(d, CH, stride=PEERS), :] = jnp.where(lane < length, near, 0.0)
        second[pl.ds(d, CH, stride=PEERS), :] = jnp.where(lane < length - LANES, far, 0.0)
        return carry

    lax.fori_loop(0, PEERS, take, 0, unroll=8)
    for c in range(CH):
        rows = slice(c * PEERS, (c + 1) * PEERS)
        near, far = first[rows, :], second[rows, :]
        both = jnp.concatenate([near, far], axis=1).astype(BF16)
        done = jnp.dot(both, toep_ref[c], preferred_element_type=F32)
        gain = skip_ref[c]
        first[rows, :] = (done[:, :LANES] + gain * near).astype(BF16).astype(F32)
        second[rows, :] = (done[:, LANES:] + gain * far).astype(BF16).astype(F32)

    def give(d, carry):
        begin, length = start_ref[d], length_ref[d]
        row = pl.multiple_of(lax.shift_right_logical(begin, 7) * CH, CH)
        turn = begin & (LANES - 1)
        near = jnp.where(lane < length, first[pl.ds(d, CH, stride=PEERS), :], 0.0)
        far = jnp.where(lane < length - LANES, second[pl.ds(d, CH, stride=PEERS), :], 0.0)
        near = pltpu.roll(near, turn, 1)
        far = pltpu.roll(far, turn, 1)
        whole = lane >= turn
        result[pl.ds(row, CH), :] += jnp.where(whole, near, 0.0)
        result[pl.ds(row + CH, CH), :] += jnp.where(whole, far, near)
        result[pl.ds(row + 2 * CH, CH), :] += jnp.where(whole, 0.0, far)
        return carry

    lax.fori_loop(0, PEERS, give, 0, unroll=8)
    for c in range(CH):
        msg[pl.ds(c, PEERS, stride=PER), :] = result[pl.ds(c, HEAD, stride=CH), :].T
    for i in range(CH // FOLD):
        parts = [result[pl.ds(HEAD * CH + FOLD * i + k, TAIL, stride=CH), :] for k in range(FOLD)]
        msg[pl.ds(CH + i, PEERS, stride=PER), :] = jnp.concatenate(parts, axis=0).T
    out_ref[...] = msg[...].astype(BF16)


def gate_kernel(in_ref, g_ref, out_ref, msg, low):
    msg[...] = in_ref[...].astype(F32)
    for i in range(CH // FOLD):
        tail = msg[pl.ds(CH + i, PEERS, stride=PER), :]
        for k in range(FOLD):
            low[pl.ds(FOLD * i + k, PEERS, stride=CH), :TAIL] = tail[:, k * TAIL : (k + 1) * TAIL]
    for j in range(8):
        cols = slice(j * LANES, (j + 1) * LANES)
        head = [msg[pl.ds((16 * j + g) * PER, CH), :] for g in range(16)]
        head = jnp.concatenate(head, axis=0).T
        head = (head * g_ref[:HEAD, cols].astype(F32)).astype(BF16)
        tail = low[cols, :].T[:TAIL]
        tail = (tail * g_ref[HEAD:, cols].astype(F32)).astype(BF16)
        for q in range(out_ref.shape[0]):
            out_ref[q, :HEAD, cols] = head
            out_ref[q, HEAD:, cols] = tail


def product_kernel(rows_ref, table_ref, out_ref, held, sems):
    blocks, size, _ = held.shape
    groups, _, width = rows_ref.shape
    copies = [
        pltpu.make_async_copy(table_ref.at[pl.ds(j * size, size)], held.at[j], sems.at[j]) for j in range(blocks)
    ]
    for copy in copies:
        copy.start()
    for j in range(blocks):
        copies[j].wait()
        total = jnp.zeros((size, ROWS), F32)
        for q in range(groups):
            part = held[j, :, q * width : (q + 1) * width]
            total += lax.dot_general(part, rows_ref[q], (((1,), (1,)), ((), ())), preferred_element_type=F32)
        out_ref[:, j * size : (j + 1) * size] = total.T.astype(BF16)


def product(rows, table):
    blocks = 4
    count, (wide, depth) = rows.shape[1], table.shape
    return pl.pallas_call(
        product_kernel,
        out_shape=jax.ShapeDtypeStruct((count, wide), BF16),
        in_specs=[full(rows.shape), pl.BlockSpec(memory_space=pltpu.HBM)],
        out_specs=full((count, wide)),
        scratch_shapes=[
            pltpu.VMEM((blocks, wide // blocks, depth), BF16),
            pltpu.SemaphoreType.DMA((blocks,)),
        ],
        compiler_params=pltpu.CompilerParams(vmem_limit_bytes=VMEM_LIMIT),
        cost_estimate=pl.CostEstimate(
            flops=2 * count * table.size,
            bytes_accessed=2 * (table.size + rows.size + count * wide),
            transcendentals=0,
        ),
    )(rows, table)


def exchange(message):
    sent = message.reshape(PEERS, PER // 2, 2, LANES)
    got = lax.all_to_all(sent, SEQ, split_axis=0, concat_axis=0, tiled=True)
    return got.reshape(MSG, LANES)


def local(values, gates, filters, skip, weights, doc_lengths):
    index = lax.axis_index(SEQ).astype(jnp.int32)
    width = values.shape[2]
    msg = jax.ShapeDtypeStruct((MSG, LANES), BF16)
    buf = pltpu.VMEM((MSG, LANES), F32)
    low = pltpu.VMEM((width, LANES), F32)
    packed = call(pack_kernel, msg, [values.reshape(ROWS, width)], [buf, low])
    table = gather_columns(weights.T)
    packed, filters, doc_lengths, skip = lax.optimization_barrier((packed, filters, doc_lengths, skip))
    toep = call(
        toeplitz_kernel,
        jax.ShapeDtypeStruct((CH, 2 * LANES, 2 * LANES), BF16),
        [index[None], filters],
        [pltpu.VMEM((LANES, 2 * LANES), F32)],
        smem=1,
    )
    starts = jnp.cumsum(doc_lengths) - doc_lengths
    own_skip = lax.dynamic_slice(skip, (index * CH,), (CH,))
    got, toep, starts, own_skip = lax.optimization_barrier((exchange(packed), toep, starts, own_skip))
    convolved = call(
        conv_kernel,
        msg,
        [starts, doc_lengths, own_skip, got, toep],
        [
            buf,
            pltpu.VMEM((MSG + 3 * CH, LANES), F32),
            pltpu.VMEM((MSG + 3 * CH, LANES), F32),
            pltpu.VMEM((CH * PEERS, LANES), F32),
            pltpu.VMEM((CH * PEERS, LANES), F32),
        ],
        flops=2 * CH * PEERS * 256 * 256,
        smem=3,
    )
    back = exchange(convolved)
    groups = lax.axis_size("chan")
    copies = call(
        gate_kernel,
        jax.ShapeDtypeStruct((groups, ROWS, width), BF16),
        [back, gates.reshape(ROWS, width)],
        [buf, low],
    )
    rows = lax.all_to_all(copies, "chan", split_axis=0, concat_axis=0, tiled=True)
    mixed = product(rows, table)
    return mixed[:, None, :]


def gather_columns(shard):
    return lax.all_gather(shard, SEQ, axis=0, tiled=True)


def solution(mesh):
    shape = dict(z=8, y=8, core=2, chan=4)
    fine = Mesh(mesh.devices.reshape(tuple(shape.values())), tuple(shape))
    placed = (
        P(None, SEQ, "chan"),
        P(None, SEQ, "chan"),
        P(None, "chan"),
        P("chan"),
        P(None, ("chan",) + SEQ),
        P(),
    )
    return jax.shard_map(
        local, mesh=fine, in_specs=placed, out_specs=P(None, SEQ, "chan"), check_vma=False
    )
```

```python
import functools

import jax
import jax.numpy as jnp
from jax import lax
from jax.experimental import pallas as pl
from jax.experimental.pallas import tpu as pltpu
from jax.sharding import Mesh
from jax.sharding import PartitionSpec as P

F32 = jnp.float32
BF16 = jnp.bfloat16
LANES = 128
CH = 8
ROWS = 160
HEAD = 128
TAIL = ROWS - HEAD
FOLD = LANES // TAIL
PER = CH + CH // FOLD
PEERS = 128
MSG = PEERS * PER
VMEM_LIMIT = 48 * 1024 * 1024
SEQ = ("z", "y_far", "y_near", "core")
NEAR = 1


def full(shape):
    return pl.BlockSpec(shape, lambda: (0,) * len(shape))


def call(kernel, out, ins, scratch, flops=0, smem=0):
    args = ins
    in_specs = [pl.BlockSpec(memory_space=pltpu.SMEM)] * smem
    in_specs += [full(a.shape) for a in args[smem:]]
    nbytes = sum(a.size * a.dtype.itemsize for a in args)
    nbytes += out.size * out.dtype.itemsize
    return pl.pallas_call(
        kernel,
        out_shape=out,
        in_specs=in_specs,
        out_specs=full(out.shape),
        scratch_shapes=scratch,
        compiler_params=pltpu.CompilerParams(vmem_limit_bytes=VMEM_LIMIT),
        cost_estimate=pl.CostEstimate(flops=flops, bytes_accessed=nbytes, transcendentals=0),
    )(*args)


def pack_kernel(v_ref, out_ref, msg, low):
    for j in range(8):
        cols = slice(j * LANES, (j + 1) * LANES)
        block = v_ref[:, cols].astype(F32)
        head = block[:HEAD].T
        for g in range(16):
            msg[pl.ds((16 * j + g) * PER, CH), :] = head[g * CH : (g + 1) * CH]
        low[cols, :TAIL] = block[HEAD:].T
    for i in range(CH // FOLD):
        parts = [low[pl.ds(FOLD * i + k, PEERS, stride=CH), :][:, :TAIL] for k in range(FOLD)]
        msg[pl.ds(CH + i, PEERS, stride=PER), :] = jnp.concatenate(parts, axis=1)
    out_ref[...] = msg[...].astype(BF16)


def toeplitz_kernel(index_ref, f_ref, out_ref, taps):
    group = index_ref[0]
    tile = pl.multiple_of(lax.div(group, 16) * LANES, LANES)
    taps[...] = f_ref[:, pl.ds(tile, LANES)].astype(F32).T
    mine = taps[pl.ds(pl.multiple_of(lax.rem(group, 16) * CH, CH), CH), :]
    row = lax.broadcasted_iota(jnp.int32, (LANES, LANES), 0)
    lane = lax.broadcasted_iota(jnp.int32, (LANES, LANES), 1)
    for c in range(CH):
        spread = jnp.broadcast_to(mine[c : c + 1, :], (LANES, 2 * LANES))
        turned = pltpu.roll(spread, 0, 1, stride=1, stride_axis=0)
        near = jnp.where(lane >= row, turned[:, :LANES], 0.0).astype(BF16)
        out_ref[c, :LANES, :LANES] = near
        out_ref[c, LANES:, LANES:] = near
        out_ref[c, :LANES, LANES:] = turned[:, LANES:].astype(BF16)
        out_ref[c, LANES:, :LANES] = jnp.zeros((LANES, LANES), BF16)


def conv_kernel(start_ref, length_ref, skip_ref, in_ref, toep_ref, out_ref, msg, seq, result, first, second):
    msg[...] = in_ref[...].astype(F32)
    for c in range(CH):
        seq[pl.ds(c, HEAD, stride=CH), :] = msg[pl.ds(c, PEERS, stride=PER), :].T
    for i in range(CH // FOLD):
        tail = msg[pl.ds(CH + i, PEERS, stride=PER), :].T
        for k in range(FOLD):
            seq[pl.ds(HEAD * CH + FOLD * i + k, TAIL, stride=CH), :] = tail[k * TAIL : (k + 1) * TAIL]
    result[...] = jnp.zeros_like(result)
    lane = lax.broadcasted_iota(jnp.int32, (CH, LANES), 1)

    def take(d, carry):
        begin, length = start_ref[d], length_ref[d]
        row = pl.multiple_of(lax.shift_right_logical(begin, 7) * CH, CH)
        turn = begin & (LANES - 1)
        back = (LANES - turn) & (LANES - 1)
        pieces = [pltpu.roll(seq[pl.ds(row + CH * i, CH), :], back, 1) for i in range(3)]
        whole = lane < LANES - turn
        near = jnp.where(whole, pieces[0], pieces[1])
        far = jnp.where(whole, pieces[1], pieces[2])
        first[pl.ds(d, CH, stride=PEERS), :] = jnp.where(lane < length, near, 0.0)
        second[pl.ds(d, CH, stride=PEERS), :] = jnp.where(lane < length - LANES, far, 0.0)
        return carry

    lax.fori_loop(0, PEERS, take, 0, unroll=8)
    for c in range(CH):
        rows = slice(c * PEERS, (c + 1) * PEERS)
        near, far = first[rows, :], second[rows, :]
        both = jnp.concatenate([near, far], axis=1).astype(BF16)
        done = jnp.dot(both, toep_ref[c], preferred_element_type=F32)
        gain = skip_ref[c]
        first[rows, :] = (done[:, :LANES] + gain * near).astype(BF16).astype(F32)
        second[rows, :] = (done[:, LANES:] + gain * far).astype(BF16).astype(F32)

    def give(d, carry):
        begin, length = start_ref[d], length_ref[d]
        row = pl.multiple_of(lax.shift_right_logical(begin, 7) * CH, CH)
        turn = begin & (LANES - 1)
        near = jnp.where(lane < length, first[pl.ds(d, CH, stride=PEERS), :], 0.0)
        far = jnp.where(lane < length - LANES, second[pl.ds(d, CH, stride=PEERS), :], 0.0)
        near = pltpu.roll(near, turn, 1)
        far = pltpu.roll(far, turn, 1)
        whole = lane >= turn
        result[pl.ds(row, CH), :] += jnp.where(whole, near, 0.0)
        result[pl.ds(row + CH, CH), :] += jnp.where(whole, far, near)
        result[pl.ds(row + 2 * CH, CH), :] += jnp.where(whole, 0.0, far)
        return carry

    lax.fori_loop(0, PEERS, give, 0, unroll=8)
    for c in range(CH):
        msg[pl.ds(c, PEERS, stride=PER), :] = result[pl.ds(c, HEAD, stride=CH), :].T
    for i in range(CH // FOLD):
        parts = [result[pl.ds(HEAD * CH + FOLD * i + k, TAIL, stride=CH), :] for k in range(FOLD)]
        msg[pl.ds(CH + i, PEERS, stride=PER), :] = jnp.concatenate(parts, axis=0).T
    out_ref[...] = msg[...].astype(BF16)


def gate_kernel(in_ref, g_ref, out_ref, msg, low):
    msg[...] = in_ref[...].astype(F32)
    for i in range(CH // FOLD):
        tail = msg[pl.ds(CH + i, PEERS, stride=PER), :]
        for k in range(FOLD):
            low[pl.ds(FOLD * i + k, PEERS, stride=CH), :TAIL] = tail[:, k * TAIL : (k + 1) * TAIL]
    for j in range(8):
        cols = slice(j * LANES, (j + 1) * LANES)
        head = [msg[pl.ds((16 * j + g) * PER, CH), :] for g in range(16)]
        head = jnp.concatenate(head, axis=0).T
        head = (head * g_ref[:HEAD, cols].astype(F32)).astype(BF16)
        tail = low[cols, :].T[:TAIL]
        tail = (tail * g_ref[HEAD:, cols].astype(F32)).astype(BF16)
        for q in range(out_ref.shape[0]):
            out_ref[q, :HEAD, cols] = head
            out_ref[q, HEAD:, cols] = tail


def product_kernel(near, rows_ref, w_ref, out_ref):
    groups, _, width = rows_ref.shape
    total = jnp.zeros((w_ref.shape[0], ROWS), F32)
    for q in range(groups):
        part = w_ref[:, q * width : (q + 1) * width]
        total += lax.dot_general(part, rows_ref[q], (((1,), (1,)), ((), ())), preferred_element_type=F32)
    for j in range(w_ref.shape[0] // LANES):
        parts = []
        for y in range(8):
            for core in range(2):
                group = 16 * j + y // near * 2 * near + core * near + y % near
                parts.append(total[group * CH : (group + 1) * CH])
        block = jnp.concatenate(parts, axis=0)
        out_ref[:, j * LANES : (j + 1) * LANES] = block.T.astype(BF16)


def product(rows, table, near):
    block = 512
    return pl.pallas_call(
        functools.partial(product_kernel, near),
        out_shape=jax.ShapeDtypeStruct((ROWS, table.shape[0]), BF16),
        grid=(table.shape[0] // block,),
        in_specs=[
            pl.BlockSpec(rows.shape, lambda j: (0, 0, 0)),
            pl.BlockSpec((block, table.shape[1]), lambda j: (j, 0)),
        ],
        out_specs=pl.BlockSpec((ROWS, block), lambda j: (0, j)),
        compiler_params=pltpu.CompilerParams(vmem_limit_bytes=VMEM_LIMIT),
        cost_estimate=pl.CostEstimate(
            flops=2 * ROWS * table.size,
            bytes_accessed=2 * (table.size + rows.size + ROWS * table.shape[0]),
            transcendentals=0,
        ),
    )(rows, table)


def exchange(message):
    sent = message.reshape(PEERS, PER // 2, 2, LANES)
    got = lax.all_to_all(sent, SEQ, split_axis=0, concat_axis=0, tiled=True)
    return got.reshape(MSG, LANES)


def local(values, gates, filters, skip, weights, doc_lengths):
    index = lax.axis_index(SEQ).astype(jnp.int32)
    width = values.shape[2]
    msg = jax.ShapeDtypeStruct((MSG, LANES), BF16)
    buf = pltpu.VMEM((MSG, LANES), F32)
    low = pltpu.VMEM((width, LANES), F32)
    packed = call(pack_kernel, msg, [values.reshape(ROWS, width)], [buf, low])
    table = gather_columns(weights.T)
    packed, filters, doc_lengths, skip = lax.optimization_barrier((packed, filters, doc_lengths, skip))
    toep = call(
        toeplitz_kernel,
        jax.ShapeDtypeStruct((CH, 2 * LANES, 2 * LANES), BF16),
        [index[None], filters],
        [pltpu.VMEM((LANES, 2 * LANES), F32)],
        smem=1,
    )
    starts = jnp.cumsum(doc_lengths) - doc_lengths
    own_skip = lax.dynamic_slice(skip, (index * CH,), (CH,))
    got, toep, starts, own_skip = lax.optimization_barrier((exchange(packed), toep, starts, own_skip))
    convolved = call(
        conv_kernel,
        msg,
        [starts, doc_lengths, own_skip, got, toep],
        [
            buf,
            pltpu.VMEM((MSG + 3 * CH, LANES), F32),
            pltpu.VMEM((MSG + 3 * CH, LANES), F32),
            pltpu.VMEM((CH * PEERS, LANES), F32),
            pltpu.VMEM((CH * PEERS, LANES), F32),
        ],
        flops=2 * CH * PEERS * 256 * 256,
        smem=3,
    )
    back = exchange(convolved)
    groups = lax.axis_size("chan")
    copies = call(
        gate_kernel,
        jax.ShapeDtypeStruct((groups, ROWS, width), BF16),
        [back, gates.reshape(ROWS, width)],
        [buf, low],
    )
    rows = lax.all_to_all(copies, "chan", split_axis=0, concat_axis=0, tiled=True)
    mixed = product(rows, table, NEAR)
    return mixed[:, None, :]


def gather_columns(shard):
    return lax.all_gather(shard, ("z", "y_far", "core"), axis=0, tiled=True)


def solution(mesh):
    shape = dict(z=8, y_far=8 // NEAR, y_near=NEAR, core=2, chan=4)
    fine = Mesh(mesh.devices.reshape(tuple(shape.values())), tuple(shape))
    placed = (
        P(None, SEQ, "chan"),
        P(None, SEQ, "chan"),
        P(None, "chan"),
        P("chan"),
        P(None, ("chan",) + SEQ),
        P(),
    )
    return jax.shard_map(
        local, mesh=fine, in_specs=placed, out_specs=P(None, SEQ, "chan"), check_vma=False
    )
```
